256 devices in a mesh: ctx: 32 (over z, x), head: 8 (over y, core).
Axes of the slice: x: 4, y: 4, z: 8, core: 2. Of those that a mesh axis runs over, the one named last changes fastest.
Arguments:
- queries: bfloat16 [4096, 3072], P(('ctx', 'head')), may hold values from -16 to 16
- keys: bfloat16 [4096, 3072], P(('ctx', 'head')), may hold values from -6 to 6
- values: bfloat16 [4096, 3072], P(('ctx', 'head')), may hold values from -6 to 6
- out_grad: bfloat16 [4096, 3072], P(('ctx', 'head')), may hold values from -6 to 6
- tile_mask: int32 [64, 64], replicated, may hold values from 0 to 1, as said below
- span_order: int32 [64], replicated, may hold values from 0 to 63, each once
Outputs:
- attended: bfloat16 [4096, 3072], P(('ctx', 'head'))
- grad_queries: bfloat16 [4096, 3072], P(('ctx', 'head'))
- grad_keys: bfloat16 [4096, 3072], P(('ctx', 'head'))
- grad_values: bfloat16 [4096, 3072], P(('ctx', 'head'))
The draws below stay inside these ranges and needn't reach their ends.
Inputs may be any that keep to these rules, and one draw needn't show every extreme that they name: tile_mask is 1 where both tiles lie in the same span of 64 tokens, 0 where the key tile's span comes later in the clip, and 0 or 1 otherwise.
All inputs are finite; a program needn't handle non-finite values.
Results may differ from the reference program's by a relative error of at most 0.04.
Values may be sent and summed in bfloat16 or wider, within the bound.
A program may use at most 64 MiB of HBM per device.

```python
import jax
import jax.numpy as jnp
from jax import lax

HEADS = 24
HD = 128
TILE = 64
TPC = 1
SPAN = 64
SPANS = 64
SEQ = 4096
TILES = 64
N_CTX = 32


def draw_queries(key, part):
    key = jax.random.fold_in(key, 11)
    drawn = jnp.clip(jax.random.normal(key, (SEQ, HEADS * HD), jnp.float32), -6.0, 6.0)
    return drawn.astype(jnp.bfloat16)


def draw_keys(key, part):
    key = jax.random.fold_in(key, 12)
    drawn = jnp.clip(jax.random.normal(key, (SEQ, HEADS * HD), jnp.float32), -6.0, 6.0)
    return drawn.astype(jnp.bfloat16)


def draw_tile_mask(key, part):
    key = jax.random.fold_in(key, 21)
    index = jnp.arange(TILES, dtype=jnp.int32)
    query_span = (index // TPC)[:, None]
    key_span = (index // TPC)[None, :]
    coins = (jax.random.randint(key, (TILES, TILES), 0, 5) < 3).astype(jnp.int32)
    inner = jnp.where(key_span < query_span, coins, 0)
    return jnp.where(key_span == query_span, 1, inner).astype(jnp.int32)


def block_scale(rng, extent, cuts, smallest, top_value):
    gain = 1.0
    for dim, shards_of in cuts:
        steps = jax.random.uniform(jax.random.fold_in(jax.random.fold_in(rng, 6), dim), (shards_of,), jnp.float32, smallest / len(cuts), top_value / len(cuts))
        gain = gain * jnp.repeat(jnp.exp(steps), extent[dim] // shards_of).reshape((-1,) + (1,) * (len(extent) - 1 - dim))
    return gain


def gaussian(own_key, extent, deviation, limit, cuts=(), kind=jnp.bfloat16):
    result = deviation * jax.random.normal(own_key, extent, jnp.float32)
    if cuts:
        result = result * block_scale(own_key, extent, cuts, -0.22, 0.18)
    return jnp.clip(result, -limit, limit).astype(kind)


def setup_inputs(seed: int = 0) -> dict:
    splits = jax.random.split(jax.random.key(seed), 7)
    return {
        "queries": draw_queries(jax.random.fold_in(splits[6], 71), 0),
        "keys": draw_keys(jax.random.fold_in(splits[6], 71), 0),
        "values": gaussian(splits[2], (SEQ, HEADS * HD), 1.0, 6.0, ((0, 256),)),
        "out_grad": gaussian(splits[3], (SEQ, HEADS * HD), 1.0, 6.0, ((0, 256),)),
        "tile_mask": draw_tile_mask(jax.random.fold_in(splits[6], 71), 0),
        "span_order": jax.random.permutation(splits[5], SPANS).astype(jnp.int32),
    }


def reference(queries, keys, values, out_grad, tile_mask, span_order):
    place = jnp.arange(SEQ, dtype=jnp.int32)
    actual = span_order[place // SPAN] * SPAN + place % SPAN
    tiles = (actual // TILE).astype(jnp.int32)
    visible = tile_mask[tiles][:, tiles] == 1
    scale = HD ** -0.5
    group_rows = SEQ // N_CTX

    def split(array):
        return array.reshape(SEQ, HEADS, HD).transpose(1, 0, 2)

    def one_head(item):
        query_h, key_h, value_h, grad_h = item
        scores = jnp.dot(query_h, key_h.T, preferred_element_type=jnp.float32) * scale
        scores = jnp.where(visible, scores, -jnp.inf)
        peak = jnp.max(scores, axis=1, keepdims=True)
        weights = jnp.where(visible, jnp.exp(scores - peak), 0.0)
        probs = weights / jnp.sum(weights, axis=1, keepdims=True)
        probs_low = probs.astype(jnp.bfloat16)
        output = jnp.dot(probs_low, value_h, preferred_element_type=jnp.float32).astype(jnp.bfloat16)
        dprob = jnp.dot(grad_h, value_h.T, preferred_element_type=jnp.float32)
        delta = jnp.sum(grad_h.astype(jnp.float32) * output.astype(jnp.float32), axis=1, keepdims=True)
        dscore = (probs * (dprob - delta)).astype(jnp.bfloat16)
        grad_query = (scale * jnp.dot(dscore, key_h, preferred_element_type=jnp.float32)).astype(jnp.bfloat16)
        score_groups = dscore.reshape(N_CTX, group_rows, SEQ).astype(jnp.float32)
        prob_groups = probs_low.reshape(N_CTX, group_rows, SEQ).astype(jnp.float32)
        query_groups = query_h.reshape(N_CTX, group_rows, HD).astype(jnp.float32)
        grad_groups = grad_h.reshape(N_CTX, group_rows, HD).astype(jnp.float32)
        key_part = (scale * jnp.einsum("cqk,cqd->ckd", score_groups, query_groups)).astype(jnp.bfloat16)
        value_part = jnp.einsum("cqk,cqd->ckd", prob_groups, grad_groups).astype(jnp.bfloat16)
        key_part, value_part = lax.optimization_barrier((key_part, value_part))
        grad_key = jnp.sum(key_part.astype(jnp.float32), axis=0).astype(jnp.bfloat16)
        grad_value = jnp.sum(value_part.astype(jnp.float32), axis=0).astype(jnp.bfloat16)
        return output, grad_query, grad_key, grad_value

    results = lax.map(one_head, (split(queries), split(keys), split(values), split(out_grad)))

    def merge(array):
        return array.transpose(1, 0, 2).reshape(SEQ, HEADS * HD)

    return (merge(results[0]), merge(results[1]), merge(results[2]), merge(results[3]))
```

```python
import functools
import math

import jax
import jax.numpy as jnp
from jax import lax
from jax.experimental import pallas as pl
from jax.experimental.pallas import tpu as pltpu
from jax.sharding import PartitionSpec as P

HD = 128
SPAN = 64
TOK = 16
NH = 3
X_CHIPS = 4
BIG = 2.0**100
FLOOR = -(2.0**80)
MESH = pl.DeviceIdType.MESH
CHUNK = 256


def dot_last(a, b):
    return lax.dot_general(a, b, (((1,), (1,)), ((), ())), preferred_element_type=jnp.float32)


def dot_first(a, b):
    return lax.dot_general(a, b, (((0,), (0,)), ((), ())), preferred_element_type=jnp.float32)


def dot(a, b):
    return lax.dot_general(a, b, (((1,), (0,)), ((), ())), preferred_element_type=jnp.float32)


def rows8(a):
    return a.reshape(a.shape[0] // 8, 8, a.shape[1])


def kernel(
    nz, nx, ny,
    q_in, k_in, v_in, g_in, mask_ref, span_ref,
    att_out, dq_out, dk_out, dv_out,
    inb, buf, key_hot, bias, probs, dprob, pb, ds, stat, oq, rq, ok, rs, xk, rx, fin, out,
    io_sem, own_sem,
    s1s, s1r, ys, yr, xs, xr, cs, cr, ts, tr, oys, oyr, ocs, ocr, oxs, oxr, zs, zr,
):
    blk = nz * TOK
    qt, kt = ny * blk, 2 * nx * blk
    chunk = min(CHUNK, kt)
    hw = NH * HD
    spans = mask_ref.shape[0]
    scale = HD**-0.5
    log2e = scale * math.log2(math.e)
    ctx, head = lax.axis_index("ctx"), lax.axis_index("head")
    z, x = ctx // nx, ctx % nx
    y, c = head // 2, head % 2
    zpeer = [(((z + j) % nz) * nx + x, head) for j in range(nz)]
    xpeer = [(z * nx + (x + j) % nx, head) for j in range(nx)]
    ypeer = [(ctx, ((y + j) % ny) * 2 + c) for j in range(ny)]
    sibling = (ctx, y * 2 + (1 - c))

    def remote(src, dst, send, recv, device):
        return pltpu.make_async_remote_copy(
            src_ref=src, dst_ref=dst, send_sem=send, recv_sem=recv,
            device_id=device, device_id_type=MESH,
        )

    def landed(dst, recv, device):
        remote(dst, dst, recv, recv, device).wait_recv()

    def columns(pos, h):
        return pl.ds(pl.multiple_of(pos * hw + h * HD, HD), HD)

    loads = [
        pltpu.make_async_copy(src, inb.at[i], io_sem.at[i])
        for i, src in enumerate((q_in, g_in, k_in, v_in))
    ]
    for load in loads:
        load.start()

    barrier = pltpu.get_barrier_semaphore()
    peers = zpeer[1:] + xpeer[1:] + ypeer[1:] + [sibling]
    for peer in peers:
        pl.semaphore_signal(barrier, inc=1, device_id=peer, device_id_type=MESH)
    pl.semaphore_wait(barrier, len(peers))
    for load in loads:
        load.wait()

    sent = []

    def go(*args):
        copy = remote(*args)
        copy.start()
        sent.append(copy)

    def scatter(h):
        for j in range(1, nz):
            go(
                inb.at[:, :, columns((z + j) % nz, h)],
                buf.at[h, :, pl.ds((nz - j) * TOK, TOK), :],
                s1s.at[h, j - 1], s1r.at[h, nz - j - 1], zpeer[j],
            )
        pltpu.make_async_copy(
            inb.at[:, :, columns(z, h)], buf.at[h, :, pl.ds(0, TOK), :], own_sem.at[h]
        ).start()

    def spread(h):
        pltpu.make_async_copy(
            inb.at[:, :, columns(z, h)], buf.at[h, :, pl.ds(0, TOK), :], own_sem.at[h]
        ).wait()
        for j in range(1, nz):
            landed(buf.at[h, :, pl.ds(j * TOK, TOK), :], s1r.at[h, j - 1], zpeer[j])
        kv = buf.at[h, pl.ds(2, 2), pl.ds(0, blk), :]
        for j in range(1, nx):
            go(
                kv, buf.at[h, pl.ds(2, 2), pl.ds((nx - j) * blk, blk), :],
                xs.at[h, j - 1], xr.at[h, nx - j - 1], xpeer[j],
            )
        qg = buf.at[h, pl.ds(0, 2), pl.ds(0, blk), :]
        for j in range(1, ny):
            go(
                qg, buf.at[h, pl.ds(0, 2), pl.ds((ny - j) * blk, blk), :],
                ys.at[h, j - 1], yr.at[h, ny - j - 1], ypeer[j],
            )
        go(
            kv, buf.at[h, pl.ds(2, 2), pl.ds(nx * blk, blk), :],
            cs.at[h, 0], cr.at[h, 0], sibling,
        )

    def forward(h):
        for j in range(1, nx):
            here = buf.at[h, pl.ds(2, 2), pl.ds(j * blk, blk), :]
            landed(here, xr.at[h, j - 1], xpeer[j])
            go(
                here, buf.at[h, pl.ds(2, 2), pl.ds((nx + j) * blk, blk), :],
                cs.at[h, j], cr.at[h, j], sibling,
            )

    def span_of(zz, xx, yy):
        return lax.div(((zz * nx + xx) * ny + yy) * 2 * TOK, SPAN)

    def mask_parts():
        tile = span_ref[...]
        picks = (lax.broadcasted_iota(jnp.int32, (spans, spans), 0) == tile).astype(jnp.bfloat16)
        table = mask_ref[...].astype(jnp.float32).astype(jnp.bfloat16)
        table = dot(table, picks).astype(jnp.bfloat16)
        table = dot_first(picks, table).astype(jnp.bfloat16)
        row = lax.broadcasted_iota(jnp.int32, (qt, spans), 0)
        slot, zz = lax.div(row, blk), lax.rem(lax.div(row, TOK), nz)
        span = span_of(lax.rem(zz + z, nz), x, lax.rem(slot + y, ny))
        hot = (lax.broadcasted_iota(jnp.int32, (qt, spans), 1) == span).astype(jnp.bfloat16)
        reach = dot(hot, table)
        bias[...] = jnp.zeros_like(bias)
        bias[:, pl.ds(0, spans)] = jnp.where(reach > 0.5, 0.0, -BIG).astype(jnp.bfloat16)
        row = lax.broadcasted_iota(jnp.int32, (kt, HD), 0)
        slot, zz = lax.rem(lax.div(row, blk), nx), lax.rem(lax.div(row, TOK), nz)
        span = span_of(lax.rem(zz + z, nz), lax.rem(slot + x, nx), y)
        key_hot[...] = (lax.broadcasted_iota(jnp.int32, (kt, HD), 1) == span).astype(
            jnp.float32
        ).astype(jnp.bfloat16)

    def first_pass(h):
        for j in range(1, ny):
            landed(buf.at[h, pl.ds(0, 2), pl.ds(j * blk, blk), :], yr.at[h, j - 1], ypeer[j])
        for j in range(nx):
            landed(buf.at[h, pl.ds(2, 2), pl.ds((nx + j) * blk, blk), :], cr.at[h, j], sibling)
        query = jnp.concatenate([buf[h, 0, pl.ds(0, qt), :], bias[...]], axis=1)

        def score(i, top):
            at = pl.ds(pl.multiple_of(i * chunk, chunk), chunk)
            key = jnp.concatenate([buf[h, 2, at, :], key_hot[at, :]], axis=1)
            s = dot_last(key, query)
            probs[h, at, :] = s
            return jnp.maximum(top, jnp.max(rows8(s), axis=0))

        top = lax.fori_loop(0, kt // chunk, score, jnp.full((8, qt), FLOOR, jnp.float32))
        top = jnp.max(top, axis=0, keepdims=True)

        def weigh(i, carry):
            total, inner = carry
            at = pl.ds(pl.multiple_of(i * chunk, chunk), chunk)
            p = jnp.exp2((probs[h, at, :] - top) * log2e)
            d = dot_last(buf[h, 3, at, :], buf[h, 1, pl.ds(0, qt), :])
            probs[h, at, :] = p
            dprob[h, at, :] = d
            return total + jnp.sum(rows8(p), axis=0), inner + jnp.sum(rows8(p * d), axis=0)

        zero = jnp.zeros((8, qt), jnp.float32)
        total, inner = lax.fori_loop(0, kt // chunk, weigh, (zero, zero))
        stat[h, 0, pl.ds(0, 1), :] = top
        stat[h, 0, pl.ds(1, 1), :] = jnp.sum(total, axis=0, keepdims=True)
        stat[h, 0, pl.ds(2, 1), :] = jnp.sum(inner, axis=0, keepdims=True)
        stat[h, 0, pl.ds(3, 5), :] = jnp.zeros((5, qt), jnp.float32)
        for j in range(1, ny):
            go(
                stat.at[h, 0], stat.at[h, ny - j],
                ts.at[h, j - 1], tr.at[h, ny - j - 1], ypeer[j],
            )

    def second_pass(h):
        for j in range(1, ny):
            landed(stat.at[h, j], tr.at[h, j - 1], ypeer[j])
        parts = [stat[h, 0]] + [
            jnp.concatenate(
                [stat[h, j, :, pl.ds(qt - j * blk, j * blk)], stat[h, j, :, pl.ds(0, qt - j * blk)]],
                axis=1,
            )
            for j in range(1, ny)
        ]
        top = functools.reduce(jnp.maximum, [s[0:1] for s in parts])
        shares = [jnp.exp2((s[0:1] - top) * log2e) for s in parts]
        total = sum(w * s[1:2] for w, s in zip(shares, parts))
        delta = sum(w * s[2:3] for w, s in zip(shares, parts)) / total
        norm = shares[0] / total

        def weigh(i, carry):
            at = pl.ds(pl.multiple_of(i * chunk, chunk), chunk)
            p = probs[h, at, :] * norm
            pb[at, :] = p.astype(jnp.bfloat16)
            ds[at, :] = (p * (dprob[h, at, :] - delta)).astype(jnp.bfloat16)
            return carry

        lax.fori_loop(0, kt // chunk, weigh, 0)
        dk = (dot(ds[...], buf[h, 0, pl.ds(0, qt), :]) * scale).astype(jnp.bfloat16)
        dv = dot(pb[...], buf[h, 1, pl.ds(0, qt), :]).astype(jnp.bfloat16)
        for core in range(2):
            for j in range(nx):
                at = (core * nx + j) * blk
                ok[h, core, j, 0] = dk[at : at + blk]
                ok[h, core, j, 1] = dv[at : at + blk]
        go(ok.at[h, 1], rs.at[h], ocs.at[h], ocr.at[h], sibling)
        att = dot_first(buf[h, 3], pb[...]).astype(jnp.bfloat16)
        dq = (dot_first(buf[h, 2], ds[...]) * scale).astype(jnp.bfloat16)
        for j in range(ny):
            oq[h, j, 0] = att[:, j * blk : (j + 1) * blk]
            oq[h, j, 1] = dq[:, j * blk : (j + 1) * blk]
        for j in range(1, ny):
            go(
                oq.at[h, j], rq.at[h, ny - j - 1],
                oys.at[h, j - 1], oyr.at[h, ny - j - 1], ypeer[j],
            )

    def core_sum(h):
        landed(rs.at[h], ocr.at[h], sibling)
        for j in range(nx):
            both = ok[h, 0, j].astype(jnp.float32) + rs[h, j].astype(jnp.float32)
            xk[h, j] = both.astype(jnp.bfloat16)
        for j in range(1, nx):
            go(
                xk.at[h, j], rx.at[h, nx - j - 1],
                oxs.at[h, j - 1], oxr.at[h, nx - j - 1], xpeer[j],
            )

    def finish(h):
        total = oq[h, 0].astype(jnp.float32)
        for j in range(1, ny):
            landed(rq.at[h, j - 1], oyr.at[h, j - 1], ypeer[j])
            total = total + rq[h, j - 1].astype(jnp.float32)
        fin[h, 0] = total[0].T.astype(jnp.bfloat16)
        fin[h, 1] = total[1].T.astype(jnp.bfloat16)
        total = xk[h, 0].astype(jnp.float32)
        for j in range(1, nx):
            landed(rx.at[h, j - 1], oxr.at[h, j - 1], xpeer[j])
            total = total + rx[h, j - 1].astype(jnp.float32)
        fin[h, 2] = total[0].astype(jnp.bfloat16)
        fin[h, 3] = total[1].astype(jnp.bfloat16)
        for j in range(1, nz):
            go(
                fin.at[h, :, pl.ds(j * TOK, TOK), :], out.at[:, :, columns(z, h)],
                zs.at[h, j - 1], zr.at[h, nz - j - 1], zpeer[j],
            )
        out[:, :, columns(z, h)] = fin[h, :, pl.ds(0, TOK), :]

    for h in range(NH):
        scatter(h)
    mask_parts()
    spread(0)
    spread(1)
    forward(0)
    spread(2)
    forward(1)
    first_pass(0)
    forward(2)
    first_pass(1)
    second_pass(0)
    first_pass(2)
    core_sum(0)
    second_pass(1)
    finish(0)
    second_pass(2)
    core_sum(1)
    finish(1)
    core_sum(2)
    finish(2)
    for h in range(NH):
        for j in range(1, nz):
            landed(out.at[:, :, columns((z + j) % nz, h)], zr.at[h, j - 1], zpeer[j])
    stores = [
        pltpu.make_async_copy(out.at[i], dst, io_sem.at[i])
        for i, dst in enumerate((att_out, dq_out, dk_out, dv_out))
    ]
    for store in stores:
        store.start()
    for copy in sent:
        copy.wait_send()
    for store in stores:
        store.wait()


def on_device(nz, nx, ny, queries, keys, values, out_grad, tile_mask, span_order):
    width = queries.shape[1]
    blk = nz * TOK
    qt, kt = ny * blk, 2 * nx * blk
    bf, f32 = jnp.bfloat16, jnp.float32
    dma = pltpu.SemaphoreType.DMA
    vmem = pl.BlockSpec(memory_space=pltpu.VMEM)
    hbm = pl.BlockSpec(memory_space=pl.ANY)
    outs = pl.pallas_call(
        functools.partial(kernel, nz, nx, ny),
        out_shape=[jax.ShapeDtypeStruct(queries.shape, bf)] * 4,
        in_specs=[hbm] * 4 + [vmem] * 2,
        out_specs=[hbm] * 4,
        scratch_shapes=[
            pltpu.VMEM((4, TOK, width), bf),
            pltpu.VMEM((NH, 4, kt, HD), bf),
            pltpu.VMEM((kt, HD), bf),
            pltpu.VMEM((qt, HD), bf),
            pltpu.VMEM((NH, kt, qt), f32),
            pltpu.VMEM((NH, kt, qt), f32),
            pltpu.VMEM((kt, qt), bf),
            pltpu.VMEM((kt, qt), bf),
            pltpu.VMEM((NH, ny, 8, qt), f32),
            pltpu.VMEM((NH, ny, 2, HD, blk), bf),
            pltpu.VMEM((NH, ny - 1, 2, HD, blk), bf),
            pltpu.VMEM((NH, 2, nx, 2, blk, HD), bf),
            pltpu.VMEM((NH, nx, 2, blk, HD), bf),
            pltpu.VMEM((NH, nx, 2, blk, HD), bf),
            pltpu.VMEM((NH, nx - 1, 2, blk, HD), bf),
            pltpu.VMEM((NH, 4, blk, HD), bf),
            pltpu.VMEM((4, TOK, width), bf),
            dma((4,)), dma((NH,)),
            dma((NH, nz - 1)), dma((NH, nz - 1)),
            dma((NH, ny - 1)), dma((NH, ny - 1)),
            dma((NH, nx - 1)), dma((NH, nx - 1)),
            dma((NH, nx)), dma((NH, nx)),
            dma((NH, ny - 1)), dma((NH, ny - 1)),
            dma((NH, ny - 1)), dma((NH, ny - 1)),
            dma((NH,)), dma((NH,)),
            dma((NH, nx - 1)), dma((NH, nx - 1)),
            dma((NH, nz - 1)), dma((NH, nz - 1)),
        ],
        compiler_params=pltpu.CompilerParams(
            collective_id=0, has_side_effects=True, vmem_limit_bytes=48 * 1024 * 1024
        ),
    )(queries, keys, values, out_grad, tile_mask, span_order.reshape(1, -1))
    return tuple(outs)


def solution(mesh, nx=X_CHIPS):
    nz, ny = mesh.shape["ctx"] // nx, mesh.shape["head"] // 2
    rows = P(("ctx", "head"), None)
    return jax.shard_map(
        functools.partial(on_device, nz, nx, ny),
        mesh=mesh,
        in_specs=(rows, rows, rows, rows, P(), P()),
        out_specs=(rows, rows, rows, rows),
        check_vma=False,
    )
```

```python
import functools
import math

import jax
import jax.numpy as jnp
from jax import lax
from jax.experimental import pallas as pl
from jax.experimental.pallas import tpu as pltpu
from jax.sharding import PartitionSpec as P

HD = 128
SPAN = 64
TOK = 16
NH = 3
X_CHIPS = 4
BIG = 2.0**100
FLOOR = -(2.0**80)
MESH = pl.DeviceIdType.MESH
CHUNK = 256


def dot_last(a, b):
    return lax.dot_general(a, b, (((1,), (1,)), ((), ())), preferred_element_type=jnp.float32)


def dot_first(a, b):
    return lax.dot_general(a, b, (((0,), (0,)), ((), ())), preferred_element_type=jnp.float32)


def dot(a, b):
    return lax.dot_general(a, b, (((1,), (0,)), ((), ())), preferred_element_type=jnp.float32)


def rows8(a):
    return a.reshape(a.shape[0] // 8, 8, a.shape[1])


def kernel(
    nz, nx, ny,
    q_in, k_in, v_in, g_in, mask_in, span_in,
    out,
    mask_ref, span_ref, inb, buf, key_hot, bias, probs, dprob, pb, ds, stat, oq, rq, ok, rs, xk, rx, fin,
    io_sem, own_sem,
    s1s, s1r, ys, yr, xs, xr, cs, cr, ts, tr, oys, oyr, ocs, ocr, oxs, oxr, zs, zr,
):
    blk = nz * TOK
    qt, kt = ny * blk, 2 * nx * blk
    chunk = min(CHUNK, kt)
    hw = NH * HD
    spans = mask_ref.shape[0]
    scale = HD**-0.5
    log2e = scale * math.log2(math.e)
    ctx, head = lax.axis_index("ctx"), lax.axis_index("head")
    z, x = ctx // nx, ctx % nx
    y, c = head // 2, head % 2
    zpeer = [(((z + j) % nz) * nx + x, head) for j in range(nz)]
    xpeer = [(z * nx + (x + j) % nx, head) for j in range(nx)]
    ypeer = [(ctx, ((y + j) % ny) * 2 + c) for j in range(ny)]
    sibling = (ctx, y * 2 + (1 - c))

    def remote(src, dst, send, recv, device):
        return pltpu.make_async_remote_copy(
            src_ref=src, dst_ref=dst, send_sem=send, recv_sem=recv,
            device_id=device, device_id_type=MESH,
        )

    def landed(dst, recv, device):
        remote(dst, dst, recv, recv, device).wait_recv()

    def columns(pos, h):
        return pl.ds(pl.multiple_of(pos * hw + h * HD, HD), HD)

    loads = [
        pltpu.make_async_copy(src, inb.at[i], io_sem.at[i])
        for i, src in enumerate((q_in, g_in, k_in, v_in))
    ]
    tables = [
        pltpu.make_async_copy(mask_in, mask_ref, io_sem.at[4]),
        pltpu.make_async_copy(span_in, span_ref, io_sem.at[5]),
    ]
    for load in loads + tables:
        load.start()

    barrier = pltpu.get_barrier_semaphore()
    peers = zpeer[1:] + xpeer[1:] + ypeer[1:] + [sibling]
    for peer in peers:
        pl.semaphore_signal(barrier, inc=1, device_id=peer, device_id_type=MESH)
    pl.semaphore_wait(barrier, len(peers))
    for load in loads:
        load.wait()

    sent = []

    def go(*args):
        copy = remote(*args)
        copy.start()
        sent.append(copy)

    def scatter(h):
        for copy in sent:
            copy.wait_send()
        sent.clear()
        for j in range(1, nz):
            go(
                inb.at[:, :, columns((z + j) % nz, h)],
                buf.at[h, :, pl.ds((nz - j) * TOK, TOK), :],
                s1s.at[h, j - 1], s1r.at[h, nz - j - 1], zpeer[j],
            )
        pltpu.make_async_copy(
            inb.at[:, :, columns(z, h)], buf.at[h, :, pl.ds(0, TOK), :], own_sem.at[h]
        ).start()

    def spread(h):
        pltpu.make_async_copy(
            inb.at[:, :, columns(z, h)], buf.at[h, :, pl.ds(0, TOK), :], own_sem.at[h]
        ).wait()
        for j in range(1, nz):
            landed(buf.at[h, :, pl.ds(j * TOK, TOK), :], s1r.at[h, j - 1], zpeer[j])
        kv = buf.at[h, pl.ds(2, 2), pl.ds(0, blk), :]
        for j in range(1, nx):
            go(
                kv, buf.at[h, pl.ds(2, 2), pl.ds((nx - j) * blk, blk), :],
                xs.at[h, j - 1], xr.at[h, nx - j - 1], xpeer[j],
            )
        qg = buf.at[h, pl.ds(0, 2), pl.ds(0, blk), :]
        for j in range(1, ny):
            go(
                qg, buf.at[h, pl.ds(0, 2), pl.ds((ny - j) * blk, blk), :],
                ys.at[h, j - 1], yr.at[h, ny - j - 1], ypeer[j],
            )
        go(
            kv, buf.at[h, pl.ds(2, 2), pl.ds(nx * blk, blk), :],
            cs.at[h, 0], cr.at[h, 0], sibling,
        )

    def forward(h):
        for j in range(1, nx):
            here = buf.at[h, pl.ds(2, 2), pl.ds(j * blk, blk), :]
            landed(here, xr.at[h, j - 1], xpeer[j])
            go(
                here, buf.at[h, pl.ds(2, 2), pl.ds((nx + j) * blk, blk), :],
                cs.at[h, j], cr.at[h, j], sibling,
            )

    def span_of(zz, xx, yy):
        return lax.div(((zz * nx + xx) * ny + yy) * 2 * TOK, SPAN)

    def mask_parts():
        tile = span_ref[...]
        picks = (lax.broadcasted_iota(jnp.int32, (spans, spans), 0) == tile).astype(jnp.bfloat16)
        table = mask_ref[...].astype(jnp.float32).astype(jnp.bfloat16)
        table = dot(table, picks).astype(jnp.bfloat16)
        table = dot_first(picks, table).astype(jnp.bfloat16)
        row = lax.broadcasted_iota(jnp.int32, (qt, spans), 0)
        slot, zz = lax.div(row, blk), lax.rem(lax.div(row, TOK), nz)
        span = span_of(lax.rem(zz + z, nz), x, lax.rem(slot + y, ny))
        hot = (lax.broadcasted_iota(jnp.int32, (qt, spans), 1) == span).astype(jnp.bfloat16)
        reach = dot(hot, table)
        bias[...] = jnp.zeros_like(bias)
        bias[:, pl.ds(0, spans)] = jnp.where(reach > 0.5, 0.0, -BIG).astype(jnp.bfloat16)
        row = lax.broadcasted_iota(jnp.int32, (kt, HD), 0)
        slot, zz = lax.rem(lax.div(row, blk), nx), lax.rem(lax.div(row, TOK), nz)
        span = span_of(lax.rem(zz + z, nz), lax.rem(slot + x, nx), y)
        key_hot[...] = (lax.broadcasted_iota(jnp.int32, (kt, HD), 1) == span).astype(
            jnp.float32
        ).astype(jnp.bfloat16)

    def first_pass(h):
        for j in range(1, ny):
            landed(buf.at[h, pl.ds(0, 2), pl.ds(j * blk, blk), :], yr.at[h, j - 1], ypeer[j])
        for j in range(nx):
            landed(buf.at[h, pl.ds(2, 2), pl.ds((nx + j) * blk, blk), :], cr.at[h, j], sibling)
        query = jnp.concatenate([buf[h, 0, pl.ds(0, qt), :], bias[...]], axis=1)

        def score(i, top):
            at = pl.ds(pl.multiple_of(i * chunk, chunk), chunk)
            key = jnp.concatenate([buf[h, 2, at, :], key_hot[at, :]], axis=1)
            s = dot_last(key, query)
            probs[h, at, :] = s
            return jnp.maximum(top, jnp.max(rows8(s), axis=0))

        top = lax.fori_loop(0, kt // chunk, score, jnp.full((8, qt), FLOOR, jnp.float32))
        top = jnp.max(top, axis=0, keepdims=True)

        def weigh(i, carry):
            total, inner = carry
            at = pl.ds(pl.multiple_of(i * chunk, chunk), chunk)
            p = jnp.exp2((probs[h, at, :] - top) * log2e)
            d = dot_last(buf[h, 3, at, :], buf[h, 1, pl.ds(0, qt), :])
            probs[h, at, :] = p
            dprob[h, at, :] = d
            return total + jnp.sum(rows8(p), axis=0), inner + jnp.sum(rows8(p * d), axis=0)

        zero = jnp.zeros((8, qt), jnp.float32)
        total, inner = lax.fori_loop(0, kt // chunk, weigh, (zero, zero))
        stat[h, 0, pl.ds(0, 1), :] = top
        stat[h, 0, pl.ds(1, 1), :] = jnp.sum(total, axis=0, keepdims=True)
        stat[h, 0, pl.ds(2, 1), :] = jnp.sum(inner, axis=0, keepdims=True)
        stat[h, 0, pl.ds(3, 5), :] = jnp.zeros((5, qt), jnp.float32)
        for j in range(1, ny):
            go(
                stat.at[h, 0], stat.at[h, ny - j],
                ts.at[h, j - 1], tr.at[h, ny - j - 1], ypeer[j],
            )

    def second_pass(h):
        for j in range(1, ny):
            landed(stat.at[h, j], tr.at[h, j - 1], ypeer[j])
        parts = [stat[h, 0]] + [
            jnp.concatenate(
                [stat[h, j, :, pl.ds(qt - j * blk, j * blk)], stat[h, j, :, pl.ds(0, qt - j * blk)]],
                axis=1,
            )
            for j in range(1, ny)
        ]
        top = functools.reduce(jnp.maximum, [s[0:1] for s in parts])
        shares = [jnp.exp2((s[0:1] - top) * log2e) for s in parts]
        total = sum(w * s[1:2] for w, s in zip(shares, parts))
        delta = sum(w * s[2:3] for w, s in zip(shares, parts)) / total
        norm = shares[0] / total

        def weigh(i, carry):
            at = pl.ds(pl.multiple_of(i * chunk, chunk), chunk)
            p = probs[h, at, :] * norm
            pb[at, :] = p.astype(jnp.bfloat16)
            ds[at, :] = (p * (dprob[h, at, :] - delta)).astype(jnp.bfloat16)
            return carry

        lax.fori_loop(0, kt // chunk, weigh, 0)
        dk = (dot(ds[...], buf[h, 0, pl.ds(0, qt), :]) * scale).astype(jnp.bfloat16)
        dv = dot(pb[...], buf[h, 1, pl.ds(0, qt), :]).astype(jnp.bfloat16)
        for core in range(2):
            for j in range(nx):
                at = (core * nx + j) * blk
                ok[h, core, j, 0] = dk[at : at + blk]
                ok[h, core, j, 1] = dv[at : at + blk]
        go(ok.at[h, 1], rs.at[h], ocs.at[h], ocr.at[h], sibling)
        att = dot_first(buf[h, 3], pb[...]).astype(jnp.bfloat16)
        dq = (dot_first(buf[h, 2], ds[...]) * scale).astype(jnp.bfloat16)
        for j in range(ny):
            oq[h, j, 0] = att[:, j * blk : (j + 1) * blk]
            oq[h, j, 1] = dq[:, j * blk : (j + 1) * blk]
        for j in range(1, ny):
            go(
                oq.at[h, j], rq.at[h, ny - j - 1],
                oys.at[h, j - 1], oyr.at[h, ny - j - 1], ypeer[j],
            )

    def core_sum(h):
        landed(rs.at[h], ocr.at[h], sibling)
        for j in range(nx):
            both = ok[h, 0, j].astype(jnp.float32) + rs[h, j].astype(jnp.float32)
            xk[h, j] = both.astype(jnp.bfloat16)
        for j in range(1, nx):
            go(
                xk.at[h, j], rx.at[h, nx - j - 1],
                oxs.at[h, j - 1], oxr.at[h, nx - j - 1], xpeer[j],
            )

    def finish(h):
        total = oq[h, 0].astype(jnp.float32)
        for j in range(1, ny):
            landed(rq.at[h, j - 1], oyr.at[h, j - 1], ypeer[j])
            total = total + rq[h, j - 1].astype(jnp.float32)
        fin[h, 0] = total[0].T.astype(jnp.bfloat16)
        fin[h, 1] = total[1].T.astype(jnp.bfloat16)
        total = xk[h, 0].astype(jnp.float32)
        for j in range(1, nx):
            landed(rx.at[h, j - 1], oxr.at[h, j - 1], xpeer[j])
            total = total + rx[h, j - 1].astype(jnp.float32)
        fin[h, 2] = total[0].astype(jnp.bfloat16)
        fin[h, 3] = total[1].astype(jnp.bfloat16)
        for j in range(1, nz):
            go(
                fin.at[h, :, pl.ds(j * TOK, TOK), :], out.at[:, :, columns(z, h)],
                zs.at[h, j - 1], zr.at[h, nz - j - 1], zpeer[j],
            )
        out[:, :, columns(z, h)] = fin[h, :, pl.ds(0, TOK), :]

    scatter(0)
    for load in tables:
        load.wait()
    mask_parts()
    scatter(1)
    ahead = list(sent)
    sent.clear()
    spread(0)
    spreads = list(sent)
    sent[:] = ahead
    scatter(2)
    sent.extend(spreads)
    spread(1)
    forward(0)
    first_pass(0)
    spread(2)
    forward(1)
    first_pass(1)
    second_pass(0)
    forward(2)
    core_sum(0)
    first_pass(2)
    second_pass(1)
    core_sum(1)
    finish(0)
    second_pass(2)
    finish(1)
    core_sum(2)
    finish(2)
    for h in range(NH):
        for j in range(1, nz):
            landed(out.at[:, :, columns((z + j) % nz, h)], zr.at[h, j - 1], zpeer[j])
    for copy in sent:
        copy.wait_send()


def deliver(done, att_out, dq_out, dk_out, dv_out, sem):
    stores = [
        pltpu.make_async_copy(done.at[i], dst, sem.at[i])
        for i, dst in enumerate((att_out, dq_out, dk_out, dv_out))
    ]
    for store in stores:
        store.start()
    for store in stores:
        store.wait()


def on_device(nz, nx, ny, queries, keys, values, out_grad, tile_mask, span_order):
    width = queries.shape[1]
    blk = nz * TOK
    qt, kt = ny * blk, 2 * nx * blk
    bf, f32 = jnp.bfloat16, jnp.float32
    dma = pltpu.SemaphoreType.DMA
    vmem = pl.BlockSpec(memory_space=pltpu.VMEM)
    hbm = pl.BlockSpec(memory_space=pltpu.HBM)
    done = pl.pallas_call(
        functools.partial(kernel, nz, nx, ny),
        out_shape=pltpu.VMEM((4, TOK, width), bf),
        in_specs=[hbm] * 6,
        out_specs=vmem,
        scratch_shapes=[
            pltpu.VMEM(tile_mask.shape, jnp.int32),
            pltpu.VMEM((1, tile_mask.shape[0]), jnp.int32),
            pltpu.VMEM((4, TOK, width), bf),
            pltpu.VMEM((NH, 4, kt, HD), bf),
            pltpu.VMEM((kt, HD), bf),
            pltpu.VMEM((qt, HD), bf),
            pltpu.VMEM((NH, kt, qt), f32),
            pltpu.VMEM((NH, kt, qt), f32),
            pltpu.VMEM((kt, qt), bf),
            pltpu.VMEM((kt, qt), bf),
            pltpu.VMEM((NH, ny, 8, qt), f32),
            pltpu.VMEM((NH, ny, 2, HD, blk), bf),
            pltpu.VMEM((NH, ny - 1, 2, HD, blk), bf),
            pltpu.VMEM((NH, 2, nx, 2, blk, HD), bf),
            pltpu.VMEM((NH, nx, 2, blk, HD), bf),
            pltpu.VMEM((NH, nx, 2, blk, HD), bf),
            pltpu.VMEM((NH, nx - 1, 2, blk, HD), bf),
            pltpu.VMEM((NH, 4, blk, HD), bf),
            dma((6,)), dma((NH,)),
            dma((NH, nz - 1)), dma((NH, nz - 1)),
            dma((NH, ny - 1)), dma((NH, ny - 1)),
            dma((NH, nx - 1)), dma((NH, nx - 1)),
            dma((NH, nx)), dma((NH, nx)),
            dma((NH, ny - 1)), dma((NH, ny - 1)),
            dma((NH, ny - 1)), dma((NH, ny - 1)),
            dma((NH,)), dma((NH,)),
            dma((NH, nx - 1)), dma((NH, nx - 1)),
            dma((NH, nz - 1)), dma((NH, nz - 1)),
        ],
        compiler_params=pltpu.CompilerParams(
            collective_id=0, has_side_effects=True, vmem_limit_bytes=48 * 1024 * 1024
        ),
    )(
        *[
            pltpu.with_memory_space_constraint(a, pltpu.HBM)
            for a in (queries, keys, values, out_grad, tile_mask, span_order.reshape(1, -1))
        ]
    )
    outs = pl.pallas_call(
        deliver,
        out_shape=[pltpu.HBM(queries.shape, bf)] * 4,
        in_specs=[pl.BlockSpec(memory_space=pl.ANY)],
        out_specs=[hbm] * 4,
        scratch_shapes=[dma((4,))],
        compiler_params=pltpu.CompilerParams(vmem_limit_bytes=1024 * 1024),
    )(pltpu.with_memory_space_constraint(done, pltpu.VMEM))
    return tuple(outs)


def solution(mesh, nx=X_CHIPS):
    nz, ny = mesh.shape["ctx"] // nx, mesh.shape["head"] // 2
    rows = P(("ctx", "head"), None)
    return jax.shard_map(
        functools.partial(on_device, nz, nx, ny),
        mesh=mesh,
        in_specs=(rows, rows, rows, rows, P(), P()),
        out_specs=(rows, rows, rows, rows),
        check_vma=False,
    )
```

```python
import functools
import math

import jax
import jax.numpy as jnp
from jax import lax
from jax.experimental import pallas as pl
from jax.experimental.pallas import tpu as pltpu
from jax.sharding import PartitionSpec as P

HD = 128
SPAN = 64
TOK = 16
NH = 3
X_CHIPS = 4
BIG = 2.0**100
FLOOR = -(2.0**80)
MESH = pl.DeviceIdType.MESH
CHUNK = 256
UNROLL = 1
ORDER = """
    V0 U0 M V1 p0 U1 q0 V2 p1 U2 q1 F0 p2 a0 q2 A0 F1 a1 A1 F2 B0 a2 K0 A2 B1 K1 B2
    X0 Y0 K2 X1 Y1 X2 Y2
"""


def dot_last(a, b):
    return lax.dot_general(a, b, (((1,), (1,)), ((), ())), preferred_element_type=jnp.float32)


def dot_first(a, b):
    return lax.dot_general(a, b, (((0,), (0,)), ((), ())), preferred_element_type=jnp.float32)


def dot(a, b):
    return lax.dot_general(a, b, (((1,), (0,)), ((), ())), preferred_element_type=jnp.float32)


def rows8(a):
    return a.reshape(a.shape[0] // 8, 8, a.shape[1])


def kernel(
    nz, nx, ny,
    q_in, k_in, v_in, g_in, mask_in, span_in,
    out,
    mask_ref, span_ref, inb, buf, key_hot, bias, probs, dprob, pb, ds, stat, oq, rq, ok, rs, xk, rx, fin,
    io_sem, own_sem,
    s1s, s1r, ys, yr, xs, xr, cs, cr, ts, tr, oys, oyr, ocs, ocr, oxs, oxr, zs, zr,
):
    blk = nz * TOK
    qt, kt = ny * blk, 2 * nx * blk
    chunk = min(CHUNK, nx * blk)
    hw = NH * HD
    spans = mask_ref.shape[0]
    scale = HD**-0.5
    log2e = scale * math.log2(math.e)
    ctx, head = lax.axis_index("ctx"), lax.axis_index("head")
    z, x = ctx // nx, ctx % nx
    y, c = head // 2, head % 2
    zpeer = [(((z + j) % nz) * nx + x, head) for j in range(nz)]
    xpeer = [(z * nx + (x + j) % nx, head) for j in range(nx)]
    ypeer = [(ctx, ((y + j) % ny) * 2 + c) for j in range(ny)]
    sibling = (ctx, y * 2 + (1 - c))

    def remote(src, dst, send, recv, device):
        return pltpu.make_async_remote_copy(
            src_ref=src, dst_ref=dst, send_sem=send, recv_sem=recv,
            device_id=device, device_id_type=MESH,
        )

    def landed(dst, recv, device):
        remote(dst, dst, recv, recv, device).wait_recv()

    def columns(pos, h):
        return pl.ds(pl.multiple_of(pos * hw + h * HD, HD), HD)

    loads = [
        pltpu.make_async_copy(src, inb.at[i], io_sem.at[i])
        for i, src in enumerate((q_in, g_in, k_in, v_in))
    ]
    tables = [
        pltpu.make_async_copy(mask_in, mask_ref, io_sem.at[4]),
        pltpu.make_async_copy(span_in, span_ref, io_sem.at[5]),
    ]
    for load in loads + tables:
        load.start()

    barrier = pltpu.get_barrier_semaphore()
    peers = zpeer[1:] + xpeer[1:] + ypeer[1:] + [sibling]
    for peer in peers:
        pl.semaphore_signal(barrier, inc=1, device_id=peer, device_id_type=MESH)
    pl.semaphore_wait(barrier, len(peers))
    for load in loads:
        load.wait()

    sent, leaving = [], []

    def go(*args):
        copy = remote(*args)
        copy.start()
        sent.append(copy)

    def own_tokens(part, h):
        return pltpu.make_async_copy(
            inb.at[pl.ds(2 * part, 2), :, columns(z, h)],
            buf.at[h, pl.ds(2 * part, 2), pl.ds(0, TOK), :],
            own_sem.at[part, h],
        )

    def scatter(part, h):
        if len(leaving) == 2:
            for copy in leaving.pop(0):
                copy.wait_send()
        piece = []
        for j in range(1, nz):
            copy = remote(
                inb.at[pl.ds(2 * part, 2), :, columns((z + j) % nz, h)],
                buf.at[h, pl.ds(2 * part, 2), pl.ds((nz - j) * TOK, TOK), :],
                s1s.at[part, h, j - 1], s1r.at[part, h, nz - j - 1], zpeer[j],
            )
            copy.start()
            piece.append(copy)
        leaving.append(piece)
        own_tokens(part, h).start()

    def gathered(part, h):
        own_tokens(part, h).wait()
        for j in range(1, nz):
            landed(
                buf.at[h, pl.ds(2 * part, 2), pl.ds(j * TOK, TOK), :],
                s1r.at[part, h, j - 1], zpeer[j],
            )
        return buf.at[h, pl.ds(2 * part, 2), pl.ds(0, blk), :]

    def spread_queries(h):
        qg = gathered(0, h)
        for j in range(1, ny):
            go(
                qg, buf.at[h, pl.ds(0, 2), pl.ds((ny - j) * blk, blk), :],
                ys.at[h, j - 1], yr.at[h, ny - j - 1], ypeer[j],
            )

    def spread_keys(h):
        kv = gathered(1, h)
        for j in range(1, nx):
            go(
                kv, buf.at[h, pl.ds(2, 2), pl.ds((nx - j) * blk, blk), :],
                xs.at[h, j - 1], xr.at[h, nx - j - 1], xpeer[j],
            )
        go(
            kv, buf.at[h, pl.ds(2, 2), pl.ds(nx * blk, blk), :],
            cs.at[h, 0], cr.at[h, 0], sibling,
        )

    def forward(h):
        for j in range(1, nx):
            here = buf.at[h, pl.ds(2, 2), pl.ds(j * blk, blk), :]
            landed(here, xr.at[h, j - 1], xpeer[j])
            go(
                here, buf.at[h, pl.ds(2, 2), pl.ds((nx + j) * blk, blk), :],
                cs.at[h, j], cr.at[h, j], sibling,
            )

    def span_of(zz, xx, yy):
        return lax.div(((zz * nx + xx) * ny + yy) * 2 * TOK, SPAN)

    def mask_parts():
        tile = span_ref[...]
        picks = (lax.broadcasted_iota(jnp.int32, (spans, spans), 0) == tile).astype(jnp.bfloat16)
        table = mask_ref[...].astype(jnp.float32).astype(jnp.bfloat16)
        table = dot(table, picks).astype(jnp.bfloat16)
        table = dot_first(picks, table).astype(jnp.bfloat16)
        row = lax.broadcasted_iota(jnp.int32, (qt, spans), 0)
        slot, zz = lax.div(row, blk), lax.rem(lax.div(row, TOK), nz)
        span = span_of(lax.rem(zz + z, nz), x, lax.rem(slot + y, ny))
        hot = (lax.broadcasted_iota(jnp.int32, (qt, spans), 1) == span).astype(jnp.bfloat16)
        reach = dot(hot, table)
        bias[...] = jnp.zeros_like(bias)
        bias[:, pl.ds(0, spans)] = jnp.where(reach > 0.5, 0.0, -BIG).astype(jnp.bfloat16)
        row = lax.broadcasted_iota(jnp.int32, (kt, HD), 0)
        slot, zz = lax.rem(lax.div(row, blk), nx), lax.rem(lax.div(row, TOK), nz)
        span = span_of(lax.rem(zz + z, nz), lax.rem(slot + x, nx), y)
        key_hot[...] = (lax.broadcasted_iota(jnp.int32, (kt, HD), 1) == span).astype(
            jnp.float32
        ).astype(jnp.bfloat16)

    half = kt // 2
    tops = {}

    def chunks(first, body, carry):
        def step(i, carry):
            return body(pl.ds(pl.multiple_of(first + i * chunk, chunk), chunk), carry)

        return lax.fori_loop(0, half // chunk, step, carry, unroll=UNROLL)

    def scores(h, first, top):
        query = jnp.concatenate([buf[h, 0, pl.ds(0, qt), :], bias[...]], axis=1)
        cotangent = buf[h, 1, pl.ds(0, qt), :]

        def body(at, top):
            key = jnp.concatenate([buf[h, 2, at, :], key_hot[at, :]], axis=1)
            s = dot_last(key, query)
            probs[h, at, :] = s
            dprob[h, at, :] = dot_last(buf[h, 3, at, :], cotangent)
            return jnp.maximum(top, jnp.max(rows8(s), axis=0))

        return chunks(first, body, top)

    def own_scores(h):
        for j in range(1, ny):
            landed(buf.at[h, pl.ds(0, 2), pl.ds(j * blk, blk), :], yr.at[h, j - 1], ypeer[j])
        tops[h] = scores(h, 0, jnp.full((8, qt), FLOOR, jnp.float32))

    def first_pass(h):
        for j in range(nx):
            landed(buf.at[h, pl.ds(2, 2), pl.ds((nx + j) * blk, blk), :], cr.at[h, j], sibling)
        top = jnp.max(scores(h, half, tops.pop(h)), axis=0, keepdims=True)

        def body(at, carry):
            total, inner = carry
            p = jnp.exp2((probs[h, at, :] - top) * log2e)
            probs[h, at, :] = p
            return (
                total + jnp.sum(rows8(p), axis=0),
                inner + jnp.sum(rows8(p * dprob[h, at, :]), axis=0),
            )

        zero = jnp.zeros((8, qt), jnp.float32)
        total, inner = chunks(half, body, chunks(0, body, (zero, zero)))
        stat[h, 0, pl.ds(0, 1), :] = top
        stat[h, 0, pl.ds(1, 1), :] = jnp.sum(total, axis=0, keepdims=True)
        stat[h, 0, pl.ds(2, 1), :] = jnp.sum(inner, axis=0, keepdims=True)
        stat[h, 0, pl.ds(3, 5), :] = jnp.zeros((5, qt), jnp.float32)
        for j in range(1, ny):
            go(
                stat.at[h, 0], stat.at[h, ny - j],
                ts.at[h, j - 1], tr.at[h, ny - j - 1], ypeer[j],
            )

    def second_pass(h):
        for j in range(1, ny):
            landed(stat.at[h, j], tr.at[h, j - 1], ypeer[j])
        parts = [stat[h, 0]] + [
            jnp.concatenate(
                [stat[h, j, :, pl.ds(qt - j * blk, j * blk)], stat[h, j, :, pl.ds(0, qt - j * blk)]],
                axis=1,
            )
            for j in range(1, ny)
        ]
        top = functools.reduce(jnp.maximum, [s[0:1] for s in parts])
        shares = [jnp.exp2((s[0:1] - top) * log2e) for s in parts]
        total = sum(w * s[1:2] for w, s in zip(shares, parts))
        delta = sum(w * s[2:3] for w, s in zip(shares, parts)) / total
        norm = shares[0] / total

        query, cotangent = buf[h, 0, pl.ds(0, qt), :], buf[h, 1, pl.ds(0, qt), :]

        def key_side(core):
            for i in range(half // chunk):
                at = pl.ds(core * half + i * chunk, chunk)
                p = probs[h, at, :] * norm
                p_low = p.astype(jnp.bfloat16)
                dscore = (p * (dprob[h, at, :] - delta)).astype(jnp.bfloat16)
                pb[at, :] = p_low
                ds[at, :] = dscore
                dk = (dot(dscore, query) * scale).astype(jnp.bfloat16)
                dv = dot(p_low, cotangent).astype(jnp.bfloat16)
                for j in range(chunk // blk):
                    ok[h, core, i * (chunk // blk) + j, 0] = dk[j * blk : (j + 1) * blk]
                    ok[h, core, i * (chunk // blk) + j, 1] = dv[j * blk : (j + 1) * blk]

        key_side(1)
        go(ok.at[h, 1], rs.at[h], ocs.at[h], ocr.at[h], sibling)
        key_side(0)
        att = dot_first(buf[h, 3], pb[...]).astype(jnp.bfloat16)
        dq = (dot_first(buf[h, 2], ds[...]) * scale).astype(jnp.bfloat16)
        for j in range(ny):
            oq[h, j, 0] = att[:, j * blk : (j + 1) * blk]
            oq[h, j, 1] = dq[:, j * blk : (j + 1) * blk]
        for j in range(1, ny):
            go(
                oq.at[h, j], rq.at[h, ny - j - 1],
                oys.at[h, j - 1], oyr.at[h, ny - j - 1], ypeer[j],
            )

    def core_sum(h):
        landed(rs.at[h], ocr.at[h], sibling)
        for j in range(nx):
            both = ok[h, 0, j].astype(jnp.float32) + rs[h, j].astype(jnp.float32)
            xk[h, j] = both.astype(jnp.bfloat16)
        for j in range(1, nx):
            go(
                xk.at[h, j], rx.at[h, nx - j - 1],
                oxs.at[h, j - 1], oxr.at[h, nx - j - 1], xpeer[j],
            )

    def hand_back(part, h):
        for j in range(1, nz):
            go(
                fin.at[h, pl.ds(2 * part, 2), pl.ds(j * TOK, TOK), :],
                out.at[pl.ds(2 * part, 2), :, columns(z, h)],
                zs.at[part, h, j - 1], zr.at[part, h, nz - j - 1], zpeer[j],
            )
        out[pl.ds(2 * part, 2), :, columns(z, h)] = fin[h, pl.ds(2 * part, 2), pl.ds(0, TOK), :]

    def finish_queries(h):
        total = oq[h, 0].astype(jnp.float32)
        for j in range(1, ny):
            landed(rq.at[h, j - 1], oyr.at[h, j - 1], ypeer[j])
            total = total + rq[h, j - 1].astype(jnp.float32)
        fin[h, 0] = total[0].T.astype(jnp.bfloat16)
        fin[h, 1] = total[1].T.astype(jnp.bfloat16)
        hand_back(0, h)

    def finish_keys(h):
        total = xk[h, 0].astype(jnp.float32)
        for j in range(1, nx):
            landed(rx.at[h, j - 1], oxr.at[h, j - 1], xpeer[j])
            total = total + rx[h, j - 1].astype(jnp.float32)
        fin[h, 2] = total[0].astype(jnp.bfloat16)
        fin[h, 3] = total[1].astype(jnp.bfloat16)
        hand_back(1, h)

    def tables_in():
        for load in tables:
            load.wait()
        mask_parts()

    steps = {
        "U": functools.partial(scatter, 0), "V": functools.partial(scatter, 1),
        "q": spread_queries, "p": spread_keys, "F": forward, "a": own_scores, "A": first_pass,
        "B": second_pass, "K": core_sum, "X": finish_queries, "Y": finish_keys,
    }
    for step in ORDER.split():
        if step == "M":
            tables_in()
        else:
            steps[step[0]](int(step[1]))
    for h in range(NH):
        for part in range(2):
            for j in range(1, nz):
                landed(
                    out.at[pl.ds(2 * part, 2), :, columns((z + j) % nz, h)],
                    zr.at[part, h, j - 1], zpeer[j],
                )
    for copy in sum(leaving, sent):
        copy.wait_send()


def deliver(done, att_out, dq_out, dk_out, dv_out, sem):
    stores = [
        pltpu.make_async_copy(done.at[i], dst, sem.at[i])
        for i, dst in enumerate((att_out, dq_out, dk_out, dv_out))
    ]
    for store in stores:
        store.start()
    for store in stores:
        store.wait()


def on_device(nz, nx, ny, queries, keys, values, out_grad, tile_mask, span_order):
    width = queries.shape[1]
    blk = nz * TOK
    qt, kt = ny * blk, 2 * nx * blk
    bf, f32 = jnp.bfloat16, jnp.float32
    dma = pltpu.SemaphoreType.DMA
    vmem = pl.BlockSpec(memory_space=pltpu.VMEM)
    hbm = pl.BlockSpec(memory_space=pltpu.HBM)
    done = pl.pallas_call(
        functools.partial(kernel, nz, nx, ny),
        out_shape=pltpu.VMEM((4, TOK, width), bf),
        in_specs=[hbm] * 6,
        out_specs=vmem,
        scratch_shapes=[
            pltpu.VMEM(tile_mask.shape, jnp.int32),
            pltpu.VMEM((1, tile_mask.shape[0]), jnp.int32),
            pltpu.VMEM((4, TOK, width), bf),
            pltpu.VMEM((NH, 4, kt, HD), bf),
            pltpu.VMEM((kt, HD), bf),
            pltpu.VMEM((qt, HD), bf),
            pltpu.VMEM((NH, kt, qt), f32),
            pltpu.VMEM((NH, kt, qt), f32),
            pltpu.VMEM((kt, qt), bf),
            pltpu.VMEM((kt, qt), bf),
            pltpu.VMEM((NH, ny, 8, qt), f32),
            pltpu.VMEM((NH, ny, 2, HD, blk), bf),
            pltpu.VMEM((NH, ny - 1, 2, HD, blk), bf),
            pltpu.VMEM((NH, 2, nx, 2, blk, HD), bf),
            pltpu.VMEM((NH, nx, 2, blk, HD), bf),
            pltpu.VMEM((NH, nx, 2, blk, HD), bf),
            pltpu.VMEM((NH, nx - 1, 2, blk, HD), bf),
            pltpu.VMEM((NH, 4, blk, HD), bf),
            dma((6,)), dma((2, NH)),
            dma((2, NH, nz - 1)), dma((2, NH, nz - 1)),
            dma((NH, ny - 1)), dma((NH, ny - 1)),
            dma((NH, nx - 1)), dma((NH, nx - 1)),
            dma((NH, nx)), dma((NH, nx)),
            dma((NH, ny - 1)), dma((NH, ny - 1)),
            dma((NH, ny - 1)), dma((NH, ny - 1)),
            dma((NH,)), dma((NH,)),
            dma((NH, nx - 1)), dma((NH, nx - 1)),
            dma((2, NH, nz - 1)), dma((2, NH, nz - 1)),
        ],
        compiler_params=pltpu.CompilerParams(
            collective_id=0, has_side_effects=True, vmem_limit_bytes=48 * 1024 * 1024
        ),
    )(
        *[
            pltpu.with_memory_space_constraint(a, pltpu.HBM)
            for a in (queries, keys, values, out_grad, tile_mask, span_order.reshape(1, -1))
        ]
    )
    outs = pl.pallas_call(
        deliver,
        out_shape=[pltpu.HBM(queries.shape, bf)] * 4,
        in_specs=[pl.BlockSpec(memory_space=pl.ANY)],
        out_specs=[hbm] * 4,
        scratch_shapes=[dma((4,))],
        compiler_params=pltpu.CompilerParams(vmem_limit_bytes=1024 * 1024),
    )(pltpu.with_memory_space_constraint(done, pltpu.VMEM))
    return tuple(outs)


def solution(mesh, nx=X_CHIPS):
    nz, ny = mesh.shape["ctx"] // nx, mesh.shape["head"] // 2
    rows = P(("ctx", "head"), None)
    return jax.shard_map(
        functools.partial(on_device, nz, nx, ny),
        mesh=mesh,
        in_specs=(rows, rows, rows, rows, P(), P()),
        out_specs=(rows, rows, rows, rows),
        check_vma=False,
    )
```

```python
import functools
import math

import jax
import jax.numpy as jnp
from jax import lax
from jax.experimental import pallas as pl
from jax.experimental.pallas import tpu as pltpu
from jax.sharding import PartitionSpec as P

HD = 128
SPAN = 64
TOK = 16
NH = 3
X_CHIPS = 4
BIG = 2.0**100
FLOOR = -(2.0**80)
MESH = pl.DeviceIdType.MESH
CHUNK = 256
UNROLL = 1
ORDER = (
    "V0", "U0", "M", "V1", "p0", "V2", "q0", "U1", "p1", "U2", "F0", "p2",
    "q1", "a0", "q2", "A0", "F1", "a1", "A1", "F2", "B0", "a2", "K0", "A2",
    "B1", "X0", "K1", "B2", "Y0", "X1", "K2", "Y1", "X2", "Y2",
)


def dot_last(a, b):
    return lax.dot_general(a, b, (((1,), (1,)), ((), ())), preferred_element_type=jnp.float32)


def dot_first(a, b):
    return lax.dot_general(a, b, (((0,), (0,)), ((), ())), preferred_element_type=jnp.float32)


def dot(a, b):
    return lax.dot_general(a, b, (((1,), (0,)), ((), ())), preferred_element_type=jnp.float32)


def rows8(a):
    return a.reshape(a.shape[0] // 8, 8, a.shape[1])


def kernel(
    nz, nx, ny,
    q_in, k_in, v_in, g_in, mask_in, span_in,
    out,
    mask_ref, span_ref, inb, buf, key_hot, bias, probs, dprob, pb, ds, stat, oq, rq, ok, rs, xk, rx, fin,
    io_sem, own_sem,
    s1s, s1r, ys, yr, xs, xr, cs, cr, ts, tr, oys, oyr, ocs, ocr, oxs, oxr, zs, zr,
):
    blk = nz * TOK
    qt, kt = ny * blk, 2 * nx * blk
    chunk = min(CHUNK, nx * blk)
    hw = NH * HD
    spans = mask_ref.shape[0]
    scale = HD**-0.5
    log2e = scale * math.log2(math.e)
    ctx, head = lax.axis_index("ctx"), lax.axis_index("head")
    z, x = ctx // nx, ctx % nx
    y, c = head // 2, head % 2
    zpeer = [(((z + j) % nz) * nx + x, head) for j in range(nz)]
    xpeer = [(z * nx + (x + j) % nx, head) for j in range(nx)]
    ypeer = [(ctx, ((y + j) % ny) * 2 + c) for j in range(ny)]
    sibling = (ctx, y * 2 + (1 - c))

    def remote(src, dst, send, recv, device):
        return pltpu.make_async_remote_copy(
            src_ref=src, dst_ref=dst, send_sem=send, recv_sem=recv,
            device_id=device, device_id_type=MESH,
        )

    def landed(dst, recv, device):
        remote(dst, dst, recv, recv, device).wait_recv()

    def columns(pos, h):
        return pl.ds(pl.multiple_of(pos * hw + h * HD, HD), HD)

    loads = [
        pltpu.make_async_copy(src, inb.at[i], io_sem.at[i])
        for i, src in enumerate((q_in, g_in, k_in, v_in))
    ]
    tables = [
        pltpu.make_async_copy(mask_in, mask_ref, io_sem.at[4]),
        pltpu.make_async_copy(span_in, span_ref, io_sem.at[5]),
    ]
    for load in loads + tables:
        load.start()

    barrier = pltpu.get_barrier_semaphore()
    peers = zpeer[1:] + xpeer[1:] + ypeer[1:] + [sibling]
    for peer in peers:
        pl.semaphore_signal(barrier, inc=1, device_id=peer, device_id_type=MESH)
    pl.semaphore_wait(barrier, len(peers))
    for load in loads:
        load.wait()

    sent, leaving = [], []

    def go(*args):
        copy = remote(*args)
        copy.start()
        sent.append(copy)

    def own_tokens(part, h):
        return pltpu.make_async_copy(
            inb.at[pl.ds(2 * part, 2), :, columns(z, h)],
            buf.at[h, pl.ds(2 * part, 2), pl.ds(0, TOK), :],
            own_sem.at[part, h],
        )

    def scatter(part, h):
        if len(leaving) == 2:
            for copy in leaving.pop(0):
                copy.wait_send()
        piece = []
        for j in range(1, nz):
            copy = remote(
                inb.at[pl.ds(2 * part, 2), :, columns((z + j) % nz, h)],
                buf.at[h, pl.ds(2 * part, 2), pl.ds((nz - j) * TOK, TOK), :],
                s1s.at[part, h, j - 1], s1r.at[part, h, nz - j - 1], zpeer[j],
            )
            copy.start()
            piece.append(copy)
        leaving.append(piece)
        own_tokens(part, h).start()

    def gathered(part, h):
        own_tokens(part, h).wait()
        for j in range(1, nz):
            landed(
                buf.at[h, pl.ds(2 * part, 2), pl.ds(j * TOK, TOK), :],
                s1r.at[part, h, j - 1], zpeer[j],
            )
        return buf.at[h, pl.ds(2 * part, 2), pl.ds(0, blk), :]

    def spread_queries(h):
        qg = gathered(0, h)
        for j in range(1, ny):
            go(
                qg, buf.at[h, pl.ds(0, 2), pl.ds((ny - j) * blk, blk), :],
                ys.at[h, j - 1], yr.at[h, ny - j - 1], ypeer[j],
            )

    def spread_keys(h):
        kv = gathered(1, h)
        for j in range(1, nx):
            go(
                kv, buf.at[h, pl.ds(2, 2), pl.ds((nx - j) * blk, blk), :],
                xs.at[h, j - 1], xr.at[h, nx - j - 1], xpeer[j],
            )
        go(
            kv, buf.at[h, pl.ds(2, 2), pl.ds(nx * blk, blk), :],
            cs.at[h, 0], cr.at[h, 0], sibling,
        )

    def forward(h):
        for j in range(1, nx):
            here = buf.at[h, pl.ds(2, 2), pl.ds(j * blk, blk), :]
            landed(here, xr.at[h, j - 1], xpeer[j])
            go(
                here, buf.at[h, pl.ds(2, 2), pl.ds((nx + j) * blk, blk), :],
                cs.at[h, j], cr.at[h, j], sibling,
            )

    def span_of(zz, xx, yy):
        return lax.div(((zz * nx + xx) * ny + yy) * 2 * TOK, SPAN)

    def mask_parts():
        tile = span_ref[...]
        picks = (lax.broadcasted_iota(jnp.int32, (spans, spans), 0) == tile).astype(jnp.bfloat16)
        table = mask_ref[...].astype(jnp.float32).astype(jnp.bfloat16)
        table = dot(table, picks).astype(jnp.bfloat16)
        table = dot_first(picks, table).astype(jnp.bfloat16)
        row = lax.broadcasted_iota(jnp.int32, (qt, spans), 0)
        slot, zz = lax.div(row, blk), lax.rem(lax.div(row, TOK), nz)
        span = span_of(lax.rem(zz + z, nz), x, lax.rem(slot + y, ny))
        hot = (lax.broadcasted_iota(jnp.int32, (qt, spans), 1) == span).astype(jnp.bfloat16)
        reach = dot(hot, table)
        bias[...] = jnp.zeros_like(bias)
        bias[:, pl.ds(0, spans)] = jnp.where(reach > 0.5, 0.0, -BIG).astype(jnp.bfloat16)
        row = lax.broadcasted_iota(jnp.int32, (kt, HD), 0)
        slot, zz = lax.rem(lax.div(row, blk), nx), lax.rem(lax.div(row, TOK), nz)
        span = span_of(lax.rem(zz + z, nz), lax.rem(slot + x, nx), y)
        key_hot[...] = (lax.broadcasted_iota(jnp.int32, (kt, HD), 1) == span).astype(
            jnp.float32
        ).astype(jnp.bfloat16)

    half = kt // 2
    tops = {}

    def chunks(first, body, carry):
        def step(i, carry):
            return body(pl.ds(pl.multiple_of(first + i * chunk, chunk), chunk), carry)

        return lax.fori_loop(0, half // chunk, step, carry, unroll=UNROLL)

    def scores(h, first, top):
        query = jnp.concatenate([buf[h, 0, pl.ds(0, qt), :], bias[...]], axis=1)
        cotangent = buf[h, 1, pl.ds(0, qt), :]

        def body(at, top):
            key = jnp.concatenate([buf[h, 2, at, :], key_hot[at, :]], axis=1)
            s = dot_last(key, query)
            probs[h, at, :] = s
            dprob[h, at, :] = dot_last(buf[h, 3, at, :], cotangent)
            return jnp.maximum(top, jnp.max(rows8(s), axis=0))

        return chunks(first, body, top)

    def own_scores(h):
        for j in range(1, ny):
            landed(buf.at[h, pl.ds(0, 2), pl.ds(j * blk, blk), :], yr.at[h, j - 1], ypeer[j])
        tops[h] = scores(h, 0, jnp.full((8, qt), FLOOR, jnp.float32))

    def first_pass(h):
        for j in range(nx):
            landed(buf.at[h, pl.ds(2, 2), pl.ds((nx + j) * blk, blk), :], cr.at[h, j], sibling)
        top = jnp.max(scores(h, half, tops.pop(h)), axis=0, keepdims=True)

        def body(at, carry):
            total, inner = carry
            p = jnp.exp2((probs[h, at, :] - top) * log2e)
            probs[h, at, :] = p
            return (
                total + jnp.sum(rows8(p), axis=0),
                inner + jnp.sum(rows8(p * dprob[h, at, :]), axis=0),
            )

        zero = jnp.zeros((8, qt), jnp.float32)
        total, inner = chunks(half, body, chunks(0, body, (zero, zero)))
        stat[h, 0, pl.ds(0, 1), :] = top
        stat[h, 0, pl.ds(1, 1), :] = jnp.sum(total, axis=0, keepdims=True)
        stat[h, 0, pl.ds(2, 1), :] = jnp.sum(inner, axis=0, keepdims=True)
        stat[h, 0, pl.ds(3, 5), :] = jnp.zeros((5, qt), jnp.float32)
        for j in range(1, ny):
            go(
                stat.at[h, 0], stat.at[h, ny - j],
                ts.at[h, j - 1], tr.at[h, ny - j - 1], ypeer[j],
            )

    def second_pass(h):
        for j in range(1, ny):
            landed(stat.at[h, j], tr.at[h, j - 1], ypeer[j])
        parts = [stat[h, 0]] + [
            jnp.concatenate(
                [stat[h, j, :, pl.ds(qt - j * blk, j * blk)], stat[h, j, :, pl.ds(0, qt - j * blk)]],
                axis=1,
            )
            for j in range(1, ny)
        ]
        top = functools.reduce(jnp.maximum, [s[0:1] for s in parts])
        shares = [jnp.exp2((s[0:1] - top) * log2e) for s in parts]
        total = sum(w * s[1:2] for w, s in zip(shares, parts))
        delta = sum(w * s[2:3] for w, s in zip(shares, parts)) / total
        norm = shares[0] / total

        query, cotangent = buf[h, 0, pl.ds(0, qt), :], buf[h, 1, pl.ds(0, qt), :]

        def key_side(core):
            for i in range(half // chunk):
                at = pl.ds(core * half + i * chunk, chunk)
                p = probs[h, at, :] * norm
                p_low = p.astype(jnp.bfloat16)
                dscore = (p * (dprob[h, at, :] - delta)).astype(jnp.bfloat16)
                pb[at, :] = p_low
                ds[at, :] = dscore
                dk = (dot(dscore, query) * scale).astype(jnp.bfloat16)
                dv = dot(p_low, cotangent).astype(jnp.bfloat16)
                for j in range(chunk // blk):
                    ok[h, core, i * (chunk // blk) + j, 0] = dk[j * blk : (j + 1) * blk]
                    ok[h, core, i * (chunk // blk) + j, 1] = dv[j * blk : (j + 1) * blk]

        key_side(1)
        go(ok.at[h, 1], rs.at[h], ocs.at[h], ocr.at[h], sibling)
        key_side(0)
        att = dot_first(buf[h, 3], pb[...]).astype(jnp.bfloat16)
        dq = (dot_first(buf[h, 2], ds[...]) * scale).astype(jnp.bfloat16)
        for j in range(ny):
            oq[h, j, 0] = att[:, j * blk : (j + 1) * blk]
            oq[h, j, 1] = dq[:, j * blk : (j + 1) * blk]
        for j in range(1, ny):
            go(
                oq.at[h, j], rq.at[h, ny - j - 1],
                oys.at[h, j - 1], oyr.at[h, ny - j - 1], ypeer[j],
            )

    def core_sum(h):
        landed(rs.at[h], ocr.at[h], sibling)
        for j in range(nx):
            both = ok[h, 0, j].astype(jnp.float32) + rs[h, j].astype(jnp.float32)
            xk[h, j] = both.astype(jnp.bfloat16)
        for j in range(1, nx):
            go(
                xk.at[h, j], rx.at[h, nx - j - 1],
                oxs.at[h, j - 1], oxr.at[h, nx - j - 1], xpeer[j],
            )

    def hand_back(part, h):
        for j in range(1, nz):
            go(
                fin.at[h, pl.ds(2 * part, 2), pl.ds(j * TOK, TOK), :],
                out.at[pl.ds(2 * part, 2), :, columns(z, h)],
                zs.at[part, h, j - 1], zr.at[part, h, nz - j - 1], zpeer[j],
            )
        out[pl.ds(2 * part, 2), :, columns(z, h)] = fin[h, pl.ds(2 * part, 2), pl.ds(0, TOK), :]

    def finish_queries(h):
        total = oq[h, 0].astype(jnp.float32)
        for j in range(1, ny):
            landed(rq.at[h, j - 1], oyr.at[h, j - 1], ypeer[j])
            total = total + rq[h, j - 1].astype(jnp.float32)
        fin[h, 0] = total[0].T.astype(jnp.bfloat16)
        fin[h, 1] = total[1].T.astype(jnp.bfloat16)
        hand_back(0, h)

    def finish_keys(h):
        total = xk[h, 0].astype(jnp.float32)
        for j in range(1, nx):
            landed(rx.at[h, j - 1], oxr.at[h, j - 1], xpeer[j])
            total = total + rx[h, j - 1].astype(jnp.float32)
        fin[h, 2] = total[0].astype(jnp.bfloat16)
        fin[h, 3] = total[1].astype(jnp.bfloat16)
        hand_back(1, h)

    def tables_in():
        for load in tables:
            load.wait()
        mask_parts()

    steps = {
        "U": functools.partial(scatter, 0), "V": functools.partial(scatter, 1),
        "q": spread_queries, "p": spread_keys, "F": forward, "a": own_scores, "A": first_pass,
        "B": second_pass, "K": core_sum, "X": finish_queries, "Y": finish_keys,
    }
    for step in ORDER:
        if step == "M":
            tables_in()
        else:
            steps[step[0]](int(step[1]))
    for h in range(NH):
        for part in range(2):
            for j in range(1, nz):
                landed(
                    out.at[pl.ds(2 * part, 2), :, columns((z + j) % nz, h)],
                    zr.at[part, h, j - 1], zpeer[j],
                )
    for copy in sum(leaving, sent):
        copy.wait_send()


def deliver(done, att_out, dq_out, dk_out, dv_out, sem):
    stores = [
        pltpu.make_async_copy(done.at[i], dst, sem.at[i])
        for i, dst in enumerate((att_out, dq_out, dk_out, dv_out))
    ]
    for store in stores:
        store.start()
    for store in stores:
        store.wait()


def on_device(nz, nx, ny, queries, keys, values, out_grad, tile_mask, span_order):
    width = queries.shape[1]
    blk = nz * TOK
    qt, kt = ny * blk, 2 * nx * blk
    bf, f32 = jnp.bfloat16, jnp.float32
    dma = pltpu.SemaphoreType.DMA
    vmem = pl.BlockSpec(memory_space=pltpu.VMEM)
    hbm = pl.BlockSpec(memory_space=pltpu.HBM)
    done = pl.pallas_call(
        functools.partial(kernel, nz, nx, ny),
        out_shape=pltpu.VMEM((4, TOK, width), bf),
        in_specs=[hbm] * 6,
        out_specs=vmem,
        scratch_shapes=[
            pltpu.VMEM(tile_mask.shape, jnp.int32),
            pltpu.VMEM((1, tile_mask.shape[0]), jnp.int32),
            pltpu.VMEM((4, TOK, width), bf),
            pltpu.VMEM((NH, 4, kt, HD), bf),
            pltpu.VMEM((kt, HD), bf),
            pltpu.VMEM((qt, HD), bf),
            pltpu.VMEM((NH, kt, qt), f32),
            pltpu.VMEM((NH, kt, qt), f32),
            pltpu.VMEM((kt, qt), bf),
            pltpu.VMEM((kt, qt), bf),
            pltpu.VMEM((NH, ny, 8, qt), f32),
            pltpu.VMEM((NH, ny, 2, HD, blk), bf),
            pltpu.VMEM((NH, ny - 1, 2, HD, blk), bf),
            pltpu.VMEM((NH, 2, nx, 2, blk, HD), bf),
            pltpu.VMEM((NH, nx, 2, blk, HD), bf),
            pltpu.VMEM((NH, nx, 2, blk, HD), bf),
            pltpu.VMEM((NH, nx - 1, 2, blk, HD), bf),
            pltpu.VMEM((NH, 4, blk, HD), bf),
            dma((6,)), dma((2, NH)),
            dma((2, NH, nz - 1)), dma((2, NH, nz - 1)),
            dma((NH, ny - 1)), dma((NH, ny - 1)),
            dma((NH, nx - 1)), dma((NH, nx - 1)),
            dma((NH, nx)), dma((NH, nx)),
            dma((NH, ny - 1)), dma((NH, ny - 1)),
            dma((NH, ny - 1)), dma((NH, ny - 1)),
            dma((NH,)), dma((NH,)),
            dma((NH, nx - 1)), dma((NH, nx - 1)),
            dma((2, NH, nz - 1)), dma((2, NH, nz - 1)),
        ],
        compiler_params=pltpu.CompilerParams(
            collective_id=0, has_side_effects=True, vmem_limit_bytes=48 * 1024 * 1024
        ),
    )(
        *[
            pltpu.with_memory_space_constraint(a, pltpu.HBM)
            for a in (queries, keys, values, out_grad, tile_mask, span_order.reshape(1, -1))
        ]
    )
    outs = pl.pallas_call(
        deliver,
        out_shape=[pltpu.HBM(queries.shape, bf)] * 4,
        in_specs=[pl.BlockSpec(memory_space=pl.ANY)],
        out_specs=[hbm] * 4,
        scratch_shapes=[dma((4,))],
        compiler_params=pltpu.CompilerParams(vmem_limit_bytes=1024 * 1024),
    )(pltpu.with_memory_space_constraint(done, pltpu.VMEM))
    return tuple(outs)


def solution(mesh, nx=X_CHIPS):
    nz, ny = mesh.shape["ctx"] // nx, mesh.shape["head"] // 2
    rows = P(("ctx", "head"), None)
    return jax.shard_map(
        functools.partial(on_device, nz, nx, ny),
        mesh=mesh,
        in_specs=(rows, rows, rows, rows, P(), P()),
        out_specs=(rows, rows, rows, rows),
        check_vma=False,
    )
```

```python
import functools
import math

import jax
import jax.numpy as jnp
from jax import lax
from jax.experimental import pallas as pl
from jax.experimental.pallas import tpu as pltpu
from jax.sharding import PartitionSpec as P

HD = 128
SPAN = 64
TOK = 16
NH = 3
X_CHIPS = 4
BIG = 2.0**100
FLOOR = -(2.0**80)
MESH = pl.DeviceIdType.MESH
CHUNK = 256
UNROLL = 2
ORDER = (
    "V0", "U0", "M", "V1", "p0", "V2", "q0", "U1", "p1", "U2", "F0", "p2",
    "q1", "a0", "q2", "A0", "F1", "a1", "A1", "F2", "B0", "a2", "K0", "A2",
    "B1", "X0", "K1", "B2", "Y0", "X1", "K2", "Y1", "X2", "Y2",
)


def dot_last(a, b):
    return lax.dot_general(a, b, (((1,), (1,)), ((), ())), preferred_element_type=jnp.float32)


def dot_first(a, b):
    return lax.dot_general(a, b, (((0,), (0,)), ((), ())), preferred_element_type=jnp.float32)


def dot(a, b):
    return lax.dot_general(a, b, (((1,), (0,)), ((), ())), preferred_element_type=jnp.float32)


def rows8(a):
    return a.reshape(a.shape[0] // 8, 8, a.shape[1])


def kernel(
    nz, nx, ny,
    q_in, k_in, v_in, g_in, mask_in, span_in,
    out,
    mask_ref, span_ref, inb, buf, key_hot, bias, probs, dprob, pb, ds, stat, oq, rq, ok, rs, xk, rx, fin,
    io_sem, own_sem,
    s1s, s1r, ys, yr, xs, xr, cs, cr, ts, tr, oys, oyr, ocs, ocr, oxs, oxr, zs, zr,
):
    blk = nz * TOK
    qt, kt = ny * blk, 2 * nx * blk
    chunk = min(CHUNK, nx * blk)
    hw = NH * HD
    spans = mask_ref.shape[0]
    scale = HD**-0.5
    log2e = scale * math.log2(math.e)
    ctx, head = lax.axis_index("ctx"), lax.axis_index("head")
    z, x = ctx // nx, ctx % nx
    y, c = head // 2, head % 2
    zpeer = [(((z + j) % nz) * nx + x, head) for j in range(nz)]
    xpeer = [(z * nx + (x + j) % nx, head) for j in range(nx)]
    ypeer = [(ctx, ((y + j) % ny) * 2 + c) for j in range(ny)]
    sibling = (ctx, y * 2 + (1 - c))

    def remote(src, dst, send, recv, device):
        return pltpu.make_async_remote_copy(
            src_ref=src, dst_ref=dst, send_sem=send, recv_sem=recv,
            device_id=device, device_id_type=MESH,
        )

    def landed(dst, recv, device):
        remote(dst, dst, recv, recv, device).wait_recv()

    def columns(pos, h):
        return pl.ds(pl.multiple_of(pos * hw + h * HD, HD), HD)

    loads = [
        pltpu.make_async_copy(src, inb.at[i], io_sem.at[i])
        for i, src in enumerate((q_in, g_in, k_in, v_in))
    ]
    tables = [
        pltpu.make_async_copy(mask_in, mask_ref, io_sem.at[4]),
        pltpu.make_async_copy(span_in, span_ref, io_sem.at[5]),
    ]
    barrier = pltpu.get_barrier_semaphore()
    peers = zpeer[1:] + xpeer[1:] + ypeer[1:] + [sibling]
    for peer in peers:
        pl.semaphore_signal(barrier, inc=1, device_id=peer, device_id_type=MESH)
    for load in loads + tables:
        load.start()
    pl.semaphore_wait(barrier, len(peers))
    for load in loads:
        load.wait()

    sent, leaving = [], []

    def go(*args):
        copy = remote(*args)
        copy.start()
        sent.append(copy)

    def own_tokens(part, h):
        return pltpu.make_async_copy(
            inb.at[pl.ds(2 * part, 2), :, columns(z, h)],
            buf.at[h, pl.ds(2 * part, 2), pl.ds(0, TOK), :],
            own_sem.at[part, h],
        )

    def scatter(part, h):
        if len(leaving) == 2:
            for copy in leaving.pop(0):
                copy.wait_send()
        piece = []
        for j in range(1, nz):
            copy = remote(
                inb.at[pl.ds(2 * part, 2), :, columns((z + j) % nz, h)],
                buf.at[h, pl.ds(2 * part, 2), pl.ds((nz - j) * TOK, TOK), :],
                s1s.at[part, h, j - 1], s1r.at[part, h, nz - j - 1], zpeer[j],
            )
            copy.start()
            piece.append(copy)
        leaving.append(piece)
        own_tokens(part, h).start()

    def gathered(part, h):
        own_tokens(part, h).wait()
        for j in range(1, nz):
            landed(
                buf.at[h, pl.ds(2 * part, 2), pl.ds(j * TOK, TOK), :],
                s1r.at[part, h, j - 1], zpeer[j],
            )
        return buf.at[h, pl.ds(2 * part, 2), pl.ds(0, blk), :]

    def spread_queries(h):
        qg = gathered(0, h)
        for j in range(1, ny):
            go(
                qg, buf.at[h, pl.ds(0, 2), pl.ds((ny - j) * blk, blk), :],
                ys.at[h, j - 1], yr.at[h, ny - j - 1], ypeer[j],
            )

    def spread_keys(h):
        kv = gathered(1, h)
        for j in range(1, nx):
            go(
                kv, buf.at[h, pl.ds(2, 2), pl.ds((nx - j) * blk, blk), :],
                xs.at[h, j - 1], xr.at[h, nx - j - 1], xpeer[j],
            )
        go(
            kv, buf.at[h, pl.ds(2, 2), pl.ds(nx * blk, blk), :],
            cs.at[h, 0], cr.at[h, 0], sibling,
        )

    def forward(h):
        for j in range(1, nx):
            here = buf.at[h, pl.ds(2, 2), pl.ds(j * blk, blk), :]
            landed(here, xr.at[h, j - 1], xpeer[j])
            go(
                here, buf.at[h, pl.ds(2, 2), pl.ds((nx + j) * blk, blk), :],
                cs.at[h, j], cr.at[h, j], sibling,
            )

    def span_of(zz, xx, yy):
        return lax.div(((zz * nx + xx) * ny + yy) * 2 * TOK, SPAN)

    def mask_parts():
        tile = span_ref[...]
        picks = (lax.broadcasted_iota(jnp.int32, (spans, spans), 0) == tile).astype(jnp.bfloat16)
        table = mask_ref[...].astype(jnp.float32).astype(jnp.bfloat16)
        table = dot(table, picks).astype(jnp.bfloat16)
        table = dot_first(picks, table).astype(jnp.bfloat16)
        row = lax.broadcasted_iota(jnp.int32, (qt, spans), 0)
        slot, zz = lax.div(row, blk), lax.rem(lax.div(row, TOK), nz)
        span = span_of(lax.rem(zz + z, nz), x, lax.rem(slot + y, ny))
        hot = (lax.broadcasted_iota(jnp.int32, (qt, spans), 1) == span).astype(jnp.bfloat16)
        reach = dot(hot, table)
        bias[...] = jnp.zeros_like(bias)
        bias[:, pl.ds(0, spans)] = jnp.where(reach > 0.5, 0.0, -BIG).astype(jnp.bfloat16)
        row = lax.broadcasted_iota(jnp.int32, (kt, HD), 0)
        slot, zz = lax.rem(lax.div(row, blk), nx), lax.rem(lax.div(row, TOK), nz)
        span = span_of(lax.rem(zz + z, nz), lax.rem(slot + x, nx), y)
        key_hot[...] = (lax.broadcasted_iota(jnp.int32, (kt, HD), 1) == span).astype(
            jnp.float32
        ).astype(jnp.bfloat16)

    half = kt // 2
    tops = {}

    def chunks(first, body, carry):
        def step(i, carry):
            return body(pl.ds(pl.multiple_of(first + i * chunk, chunk), chunk), carry)

        return lax.fori_loop(0, half // chunk, step, carry, unroll=UNROLL)

    def scores(h, first, top):
        query = jnp.concatenate([buf[h, 0, pl.ds(0, qt), :], bias[...]], axis=1)
        cotangent = buf[h, 1, pl.ds(0, qt), :]

        def body(at, top):
            key = jnp.concatenate([buf[h, 2, at, :], key_hot[at, :]], axis=1)
            s = dot_last(key, query)
            probs[h, at, :] = s
            dprob[h, at, :] = dot_last(buf[h, 3, at, :], cotangent)
            return jnp.maximum(top, jnp.max(rows8(s), axis=0))

        return chunks(first, body, top)

    def own_scores(h):
        for j in range(1, ny):
            landed(buf.at[h, pl.ds(0, 2), pl.ds(j * blk, blk), :], yr.at[h, j - 1], ypeer[j])
        tops[h] = scores(h, 0, jnp.full((8, qt), FLOOR, jnp.float32))

    def first_pass(h):
        for j in range(nx):
            landed(buf.at[h, pl.ds(2, 2), pl.ds((nx + j) * blk, blk), :], cr.at[h, j], sibling)
        top = jnp.max(scores(h, half, tops.pop(h)), axis=0, keepdims=True)

        def body(at, carry):
            total, inner = carry
            p = jnp.exp2((probs[h, at, :] - top) * log2e)
            probs[h, at, :] = p
            return (
                total + jnp.sum(rows8(p), axis=0),
                inner + jnp.sum(rows8(p * dprob[h, at, :]), axis=0),
            )

        zero = jnp.zeros((8, qt), jnp.float32)
        total, inner = chunks(half, body, chunks(0, body, (zero, zero)))
        stat[h, 0, pl.ds(0, 1), :] = top
        stat[h, 0, pl.ds(1, 1), :] = jnp.sum(total, axis=0, keepdims=True)
        stat[h, 0, pl.ds(2, 1), :] = jnp.sum(inner, axis=0, keepdims=True)
        stat[h, 0, pl.ds(3, 5), :] = jnp.zeros((5, qt), jnp.float32)
        for j in range(1, ny):
            go(
                stat.at[h, 0], stat.at[h, ny - j],
                ts.at[h, j - 1], tr.at[h, ny - j - 1], ypeer[j],
            )

    def second_pass(h):
        for j in range(1, ny):
            landed(stat.at[h, j], tr.at[h, j - 1], ypeer[j])
        parts = [stat[h, 0]] + [
            jnp.concatenate(
                [stat[h, j, :, pl.ds(qt - j * blk, j * blk)], stat[h, j, :, pl.ds(0, qt - j * blk)]],
                axis=1,
            )
            for j in range(1, ny)
        ]
        top = functools.reduce(jnp.maximum, [s[0:1] for s in parts])
        shares = [jnp.exp2((s[0:1] - top) * log2e) for s in parts]
        total = sum(w * s[1:2] for w, s in zip(shares, parts))
        delta = sum(w * s[2:3] for w, s in zip(shares, parts)) / total
        norm = shares[0] / total

        query, cotangent = buf[h, 0, pl.ds(0, qt), :], buf[h, 1, pl.ds(0, qt), :]

        def key_side(core):
            for i in range(half // chunk):
                at = pl.ds(core * half + i * chunk, chunk)
                p = probs[h, at, :] * norm
                p_low = p.astype(jnp.bfloat16)
                dscore = (p * (dprob[h, at, :] - delta)).astype(jnp.bfloat16)
                pb[at, :] = p_low
                ds[at, :] = dscore
                dk = (dot(dscore, query) * scale).astype(jnp.bfloat16)
                dv = dot(p_low, cotangent).astype(jnp.bfloat16)
                for j in range(chunk // blk):
                    ok[h, core, i * (chunk // blk) + j, 0] = dk[j * blk : (j + 1) * blk]
                    ok[h, core, i * (chunk // blk) + j, 1] = dv[j * blk : (j + 1) * blk]

        key_side(1)
        go(ok.at[h, 1], rs.at[h], ocs.at[h], ocr.at[h], sibling)
        key_side(0)
        att = dot_first(buf[h, 3], pb[...]).astype(jnp.bfloat16)
        dq = (dot_first(buf[h, 2], ds[...]) * scale).astype(jnp.bfloat16)
        for j in range(ny):
            oq[h, j, 0] = att[:, j * blk : (j + 1) * blk]
            oq[h, j, 1] = dq[:, j * blk : (j + 1) * blk]
        for j in range(1, ny):
            go(
                oq.at[h, j], rq.at[h, ny - j - 1],
                oys.at[h, j - 1], oyr.at[h, ny - j - 1], ypeer[j],
            )

    def core_sum(h):
        landed(rs.at[h], ocr.at[h], sibling)
        for j in range(nx):
            both = ok[h, 0, j].astype(jnp.float32) + rs[h, j].astype(jnp.float32)
            xk[h, j] = both.astype(jnp.bfloat16)
        for j in range(1, nx):
            go(
                xk.at[h, j], rx.at[h, nx - j - 1],
                oxs.at[h, j - 1], oxr.at[h, nx - j - 1], xpeer[j],
            )

    def hand_back(part, h):
        for j in range(1, nz):
            go(
                fin.at[h, pl.ds(2 * part, 2), pl.ds(j * TOK, TOK), :],
                out.at[pl.ds(2 * part, 2), :, columns(z, h)],
                zs.at[part, h, j - 1], zr.at[part, h, nz - j - 1], zpeer[j],
            )
        out[pl.ds(2 * part, 2), :, columns(z, h)] = fin[h, pl.ds(2 * part, 2), pl.ds(0, TOK), :]

    def finish_queries(h):
        total = oq[h, 0].astype(jnp.float32)
        for j in range(1, ny):
            landed(rq.at[h, j - 1], oyr.at[h, j - 1], ypeer[j])
            total = total + rq[h, j - 1].astype(jnp.float32)
        fin[h, 0] = total[0].T.astype(jnp.bfloat16)
        fin[h, 1] = total[1].T.astype(jnp.bfloat16)
        hand_back(0, h)

    def finish_keys(h):
        total = xk[h, 0].astype(jnp.float32)
        for j in range(1, nx):
            landed(rx.at[h, j - 1], oxr.at[h, j - 1], xpeer[j])
            total = total + rx[h, j - 1].astype(jnp.float32)
        fin[h, 2] = total[0].astype(jnp.bfloat16)
        fin[h, 3] = total[1].astype(jnp.bfloat16)
        hand_back(1, h)

    def tables_in():
        for load in tables:
            load.wait()
        mask_parts()

    steps = {
        "U": functools.partial(scatter, 0), "V": functools.partial(scatter, 1),
        "q": spread_queries, "p": spread_keys, "F": forward, "a": own_scores, "A": first_pass,
        "B": second_pass, "K": core_sum, "X": finish_queries, "Y": finish_keys,
    }
    for step in ORDER:
        if step == "M":
            tables_in()
        else:
            steps[step[0]](int(step[1]))
    for copy in sum(leaving, sent):
        copy.wait_send()
    for h in range(NH):
        for part in range(2):
            for j in range(1, nz):
                landed(
                    out.at[pl.ds(2 * part, 2), :, columns((z + j) % nz, h)],
                    zr.at[part, h, j - 1], zpeer[j],
                )


def deliver(done, att_out, dq_out, dk_out, dv_out, sem):
    stores = [
        pltpu.make_async_copy(done.at[i], dst, sem.at[i])
        for i, dst in enumerate((att_out, dq_out, dk_out, dv_out))
    ]
    for store in stores:
        store.start()
    for store in stores:
        store.wait()


def on_device(nz, nx, ny, queries, keys, values, out_grad, tile_mask, span_order):
    width = queries.shape[1]
    blk = nz * TOK
    qt, kt = ny * blk, 2 * nx * blk
    bf, f32 = jnp.bfloat16, jnp.float32
    dma = pltpu.SemaphoreType.DMA
    vmem = pl.BlockSpec(memory_space=pltpu.VMEM)
    hbm = pl.BlockSpec(memory_space=pltpu.HBM)
    done = pl.pallas_call(
        functools.partial(kernel, nz, nx, ny),
        out_shape=pltpu.VMEM((4, TOK, width), bf),
        in_specs=[hbm] * 6,
        out_specs=vmem,
        scratch_shapes=[
            pltpu.VMEM(tile_mask.shape, jnp.int32),
            pltpu.VMEM((1, tile_mask.shape[0]), jnp.int32),
            pltpu.VMEM((4, TOK, width), bf),
            pltpu.VMEM((NH, 4, kt, HD), bf),
            pltpu.VMEM((kt, HD), bf),
            pltpu.VMEM((qt, HD), bf),
            pltpu.VMEM((NH, kt, qt), f32),
            pltpu.VMEM((NH, kt, qt), f32),
            pltpu.VMEM((kt, qt), bf),
            pltpu.VMEM((kt, qt), bf),
            pltpu.VMEM((NH, ny, 8, qt), f32),
            pltpu.VMEM((NH, ny, 2, HD, blk), bf),
            pltpu.VMEM((NH, ny - 1, 2, HD, blk), bf),
            pltpu.VMEM((NH, 2, nx, 2, blk, HD), bf),
            pltpu.VMEM((NH, nx, 2, blk, HD), bf),
            pltpu.VMEM((NH, nx, 2, blk, HD), bf),
            pltpu.VMEM((NH, nx - 1, 2, blk, HD), bf),
            pltpu.VMEM((NH, 4, blk, HD), bf),
            dma((6,)), dma((2, NH)),
            dma((2, NH, nz - 1)), dma((2, NH, nz - 1)),
            dma((NH, ny - 1)), dma((NH, ny - 1)),
            dma((NH, nx - 1)), dma((NH, nx - 1)),
            dma((NH, nx)), dma((NH, nx)),
            dma((NH, ny - 1)), dma((NH, ny - 1)),
            dma((NH, ny - 1)), dma((NH, ny - 1)),
            dma((NH,)), dma((NH,)),
            dma((NH, nx - 1)), dma((NH, nx - 1)),
            dma((2, NH, nz - 1)), dma((2, NH, nz - 1)),
        ],
        compiler_params=pltpu.CompilerParams(
            collective_id=0, has_side_effects=True, vmem_limit_bytes=48 * 1024 * 1024
        ),
    )(
        *[
            pltpu.with_memory_space_constraint(a, pltpu.HBM)
            for a in (queries, keys, values, out_grad, tile_mask, span_order.reshape(1, -1))
        ]
    )
    outs = pl.pallas_call(
        deliver,
        out_shape=[pltpu.HBM(queries.shape, bf)] * 4,
        in_specs=[pl.BlockSpec(memory_space=pl.ANY)],
        out_specs=[hbm] * 4,
        scratch_shapes=[dma((4,))],
        compiler_params=pltpu.CompilerParams(vmem_limit_bytes=1024 * 1024),
    )(pltpu.with_memory_space_constraint(done, pltpu.VMEM))
    return tuple(outs)


def solution(mesh, nx=X_CHIPS):
    nz, ny = mesh.shape["ctx"] // nx, mesh.shape["head"] // 2
    rows = P(("ctx", "head"), None)
    return jax.shard_map(
        functools.partial(on_device, nz, nx, ny),
        mesh=mesh,
        in_specs=(rows, rows, rows, rows, P(), P()),
        out_specs=(rows, rows, rows, rows),
        check_vma=False,
    )
```

```python
import functools
import math

import jax
import jax.numpy as jnp
from jax import lax
from jax.experimental import pallas as pl
from jax.experimental.pallas import tpu as pltpu
from jax.sharding import PartitionSpec as P

HD = 128
SPAN = 64
TOK = 16
NH = 3
X_CHIPS = 4
BIG = 2.0**100
FLOOR = -(2.0**80)
MESH = pl.DeviceIdType.MESH
CHUNK = 256
UNROLL = 2
ORDER = (
    "V0", "U0", "M", "V1", "p0", "V2", "q0", "U1", "p1", "U2", "F0", "p2",
    "q1", "a0", "q2", "A0", "F1", "a1", "A1", "F2", "B0", "a2", "K0", "A2",
    "B1", "X0", "K1", "B2", "Y0", "X1", "K2", "Y1", "X2", "Y2",
)


def dot_last(a, b):
    return lax.dot_general(a, b, (((1,), (1,)), ((), ())), preferred_element_type=jnp.float32)


def dot_first(a, b):
    return lax.dot_general(a, b, (((0,), (0,)), ((), ())), preferred_element_type=jnp.float32)


def dot(a, b):
    return lax.dot_general(a, b, (((1,), (0,)), ((), ())), preferred_element_type=jnp.float32)


def rows8(a):
    return a.reshape(a.shape[0] // 8, 8, a.shape[1])


def kernel(
    nz, nx, ny,
    q_in, k_in, v_in, g_in, mask_in, span_in,
    out,
    mask_ref, span_ref, inb, buf, key_hot, bias, probs, dprob, pb, ds, stat, oq, rq, ok, rs, xk, rx, fin,
    io_sem, own_sem,
    s1s, s1r, ys, yr, xs, xr, cs, cr, ts, tr, oys, oyr, ocs, ocr, oxs, oxr, zs, zr,
):
    blk = nz * TOK
    qt, kt = ny * blk, 2 * nx * blk
    chunk = min(CHUNK, nx * blk)
    hw = NH * HD
    spans = mask_ref.shape[0]
    scale = HD**-0.5
    log2e = scale * math.log2(math.e)
    ctx, head = lax.axis_index("ctx"), lax.axis_index("head")
    z, x = ctx // nx, ctx % nx
    y, c = head // 2, head % 2
    zpeer = [(((z + j) % nz) * nx + x, head) for j in range(nz)]
    xpeer = [(z * nx + (x + j) % nx, head) for j in range(nx)]
    ypeer = [(ctx, ((y + j) % ny) * 2 + c) for j in range(ny)]
    sibling = (ctx, y * 2 + (1 - c))

    def remote(src, dst, send, recv, device):
        return pltpu.make_async_remote_copy(
            src_ref=src, dst_ref=dst, send_sem=send, recv_sem=recv,
            device_id=device, device_id_type=MESH,
        )

    def landed(dst, recv, device):
        remote(dst, dst, recv, recv, device).wait_recv()

    def columns(pos, h):
        return pl.ds(pl.multiple_of(pos * hw + h * HD, HD), HD)

    loads = [
        pltpu.make_async_copy(src, inb.at[i], io_sem.at[i])
        for i, src in enumerate((q_in, g_in, k_in, v_in))
    ]
    tables = [
        pltpu.make_async_copy(mask_in, mask_ref, io_sem.at[4]),
        pltpu.make_async_copy(span_in, span_ref, io_sem.at[5]),
    ]
    barrier = pltpu.get_barrier_semaphore()
    peers = zpeer[1:] + xpeer[1:] + ypeer[1:] + [sibling]
    for peer in peers:
        pl.semaphore_signal(barrier, inc=1, device_id=peer, device_id_type=MESH)
    for load in loads + tables:
        load.start()
    pl.semaphore_wait(barrier, len(peers))
    for load in loads:
        load.wait()

    sent, leaving = [], []

    def go(*args):
        copy = remote(*args)
        copy.start()
        sent.append(copy)

    def own_tokens(part, h):
        return pltpu.make_async_copy(
            inb.at[pl.ds(2 * part, 2), :, columns(z, h)],
            buf.at[h, pl.ds(2 * part, 2), pl.ds(0, TOK), :],
            own_sem.at[part, h],
        )

    def scatter(part, h):
        if len(leaving) == 2:
            for copy in leaving.pop(0):
                copy.wait_send()
        piece = []
        for j in range(1, nz):
            copy = remote(
                inb.at[pl.ds(2 * part, 2), :, columns((z + j) % nz, h)],
                buf.at[h, pl.ds(2 * part, 2), pl.ds((nz - j) * TOK, TOK), :],
                s1s.at[part, h, j - 1], s1r.at[part, h, nz - j - 1], zpeer[j],
            )
            copy.start()
            piece.append(copy)
        leaving.append(piece)
        own_tokens(part, h).start()

    def gathered(part, h):
        own_tokens(part, h).wait()
        for j in range(1, nz):
            landed(
                buf.at[h, pl.ds(2 * part, 2), pl.ds(j * TOK, TOK), :],
                s1r.at[part, h, j - 1], zpeer[j],
            )
        return buf.at[h, pl.ds(2 * part, 2), pl.ds(0, blk), :]

    def spread_queries(h):
        qg = gathered(0, h)
        for j in range(1, ny):
            go(
                qg, buf.at[h, pl.ds(0, 2), pl.ds((ny - j) * blk, blk), :],
                ys.at[h, j - 1], yr.at[h, ny - j - 1], ypeer[j],
            )

    def spread_keys(h):
        kv = gathered(1, h)
        for j in range(1, nx):
            go(
                kv, buf.at[h, pl.ds(2, 2), pl.ds((nx - j) * blk, blk), :],
                xs.at[h, j - 1], xr.at[h, nx - j - 1], xpeer[j],
            )
        go(
            kv, buf.at[h, pl.ds(2, 2), pl.ds(nx * blk, blk), :],
            cs.at[h, 0], cr.at[h, 0], sibling,
        )

    def forward(h):
        for j in range(1, nx):
            here = buf.at[h, pl.ds(2, 2), pl.ds(j * blk, blk), :]
            landed(here, xr.at[h, j - 1], xpeer[j])
            go(
                here, buf.at[h, pl.ds(2, 2), pl.ds((nx + j) * blk, blk), :],
                cs.at[h, j], cr.at[h, j], sibling,
            )

    def span_of(zz, xx, yy):
        return lax.div(((zz * nx + xx) * ny + yy) * 2 * TOK, SPAN)

    def mask_parts():
        tile = span_ref[...]
        picks = (lax.broadcasted_iota(jnp.int32, (spans, spans), 0) == tile).astype(jnp.bfloat16)
        table = mask_ref[...].astype(jnp.float32).astype(jnp.bfloat16)
        table = dot(table, picks).astype(jnp.bfloat16)
        table = dot_first(picks, table).astype(jnp.bfloat16)
        row = lax.broadcasted_iota(jnp.int32, (qt, spans), 0)
        slot, zz = lax.div(row, blk), lax.rem(lax.div(row, TOK), nz)
        span = span_of(lax.rem(zz + z, nz), x, lax.rem(slot + y, ny))
        hot = (lax.broadcasted_iota(jnp.int32, (qt, spans), 1) == span).astype(jnp.bfloat16)
        reach = dot(hot, table)
        bias[...] = jnp.zeros_like(bias)
        bias[:, pl.ds(0, spans)] = jnp.where(reach > 0.5, 0.0, -BIG).astype(jnp.bfloat16)
        row = lax.broadcasted_iota(jnp.int32, (kt, HD), 0)
        slot, zz = lax.rem(lax.div(row, blk), nx), lax.rem(lax.div(row, TOK), nz)
        span = span_of(lax.rem(zz + z, nz), lax.rem(slot + x, nx), y)
        key_hot[...] = (lax.broadcasted_iota(jnp.int32, (kt, HD), 1) == span).astype(
            jnp.float32
        ).astype(jnp.bfloat16)

    half = kt // 2
    tops = {}

    def chunks(first, body, carry):
        def step(i, carry):
            return body(pl.ds(pl.multiple_of(first + i * chunk, chunk), chunk), carry)

        return lax.fori_loop(0, half // chunk, step, carry, unroll=UNROLL)

    def scores(h, first, top):
        query = jnp.concatenate([buf[h, 0, pl.ds(0, qt), :], bias[...]], axis=1)
        cotangent = buf[h, 1, pl.ds(0, qt), :]

        def body(at, top):
            key = jnp.concatenate([buf[h, 2, at, :], key_hot[at, :]], axis=1)
            s = dot_last(key, query)
            probs[h, at, :] = s
            dprob[h, at, :] = dot_last(buf[h, 3, at, :], cotangent)
            return jnp.maximum(top, jnp.max(rows8(s), axis=0))

        return chunks(first, body, top)

    def own_scores(h):
        for j in range(1, ny):
            landed(buf.at[h, pl.ds(0, 2), pl.ds(j * blk, blk), :], yr.at[h, j - 1], ypeer[j])
        tops[h] = scores(h, 0, jnp.full((8, qt), FLOOR, jnp.float32))

    def first_pass(h):
        for j in range(nx):
            landed(buf.at[h, pl.ds(2, 2), pl.ds((nx + j) * blk, blk), :], cr.at[h, j], sibling)
        top = jnp.max(scores(h, half, tops.pop(h)), axis=0, keepdims=True)

        def body(at, carry):
            total, inner = carry
            p = jnp.exp2((probs[h, at, :] - top) * log2e)
            probs[h, at, :] = p
            return (
                total + jnp.sum(rows8(p), axis=0),
                inner + jnp.sum(rows8(p * dprob[h, at, :]), axis=0),
            )

        zero = jnp.zeros((8, qt), jnp.float32)
        total, inner = chunks(half, body, chunks(0, body, (zero, zero)))
        total, inner = [jnp.sum(a, axis=0, keepdims=True) for a in (total, inner)]
        rows = [a[:, k * blk : (k + 1) * blk] for a in (top, total, inner) for k in range(ny)]
        rows += [jnp.zeros((stat.shape[2] - 3 * ny, blk), jnp.float32)]
        stat[h, 0] = jnp.concatenate(rows, axis=0)
        for j in range(1, ny):
            go(
                stat.at[h, 0], stat.at[h, ny - j],
                ts.at[h, j - 1], tr.at[h, ny - j - 1], ypeer[j],
            )

    def second_pass(h):
        for j in range(1, ny):
            landed(stat.at[h, j], tr.at[h, j - 1], ypeer[j])
        def rows(j, kind):
            return jnp.concatenate(
                [stat[h, j, pl.ds(kind * ny + (k - j) % ny, 1), :] for k in range(ny)], axis=1
            )

        peaks = [rows(j, 0) for j in range(ny)]
        top = functools.reduce(jnp.maximum, peaks)
        shares = [jnp.exp2((peak - top) * log2e) for peak in peaks]
        total = sum(w * rows(j, 1) for j, w in enumerate(shares))
        delta = sum(w * rows(j, 2) for j, w in enumerate(shares)) / total
        norm = shares[0] / total

        query, cotangent = buf[h, 0, pl.ds(0, qt), :], buf[h, 1, pl.ds(0, qt), :]

        def key_side(core):
            for i in range(half // chunk):
                at = pl.ds(core * half + i * chunk, chunk)
                p = probs[h, at, :] * norm
                p_low = p.astype(jnp.bfloat16)
                dscore = (p * (dprob[h, at, :] - delta)).astype(jnp.bfloat16)
                pb[at, :] = p_low
                ds[at, :] = dscore
                dk = (dot(dscore, query) * scale).astype(jnp.bfloat16)
                dv = dot(p_low, cotangent).astype(jnp.bfloat16)
                for j in range(chunk // blk):
                    ok[h, core, i * (chunk // blk) + j, 0] = dk[j * blk : (j + 1) * blk]
                    ok[h, core, i * (chunk // blk) + j, 1] = dv[j * blk : (j + 1) * blk]

        key_side(1)
        go(ok.at[h, 1], rs.at[h], ocs.at[h], ocr.at[h], sibling)
        key_side(0)
        att = dot_first(buf[h, 3], pb[...]).astype(jnp.bfloat16)
        dq = (dot_first(buf[h, 2], ds[...]) * scale).astype(jnp.bfloat16)
        for j in range(ny):
            oq[h, j, 0] = att[:, j * blk : (j + 1) * blk]
            oq[h, j, 1] = dq[:, j * blk : (j + 1) * blk]
        for j in range(1, ny):
            go(
                oq.at[h, j], rq.at[h, ny - j - 1],
                oys.at[h, j - 1], oyr.at[h, ny - j - 1], ypeer[j],
            )

    def core_sum(h):
        landed(rs.at[h], ocr.at[h], sibling)
        for j in range(nx):
            both = ok[h, 0, j].astype(jnp.float32) + rs[h, j].astype(jnp.float32)
            xk[h, j] = both.astype(jnp.bfloat16)
        for j in range(1, nx):
            go(
                xk.at[h, j], rx.at[h, nx - j - 1],
                oxs.at[h, j - 1], oxr.at[h, nx - j - 1], xpeer[j],
            )

    def hand_back(part, h):
        for j in range(1, nz):
            go(
                fin.at[h, pl.ds(2 * part, 2), pl.ds(j * TOK, TOK), :],
                out.at[pl.ds(2 * part, 2), :, columns(z, h)],
                zs.at[part, h, j - 1], zr.at[part, h, nz - j - 1], zpeer[j],
            )
        out[pl.ds(2 * part, 2), :, columns(z, h)] = fin[h, pl.ds(2 * part, 2), pl.ds(0, TOK), :]

    def finish_queries(h):
        total = oq[h, 0].astype(jnp.float32)
        for j in range(1, ny):
            landed(rq.at[h, j - 1], oyr.at[h, j - 1], ypeer[j])
            total = total + rq[h, j - 1].astype(jnp.float32)
        fin[h, 0] = total[0].T.astype(jnp.bfloat16)
        fin[h, 1] = total[1].T.astype(jnp.bfloat16)
        hand_back(0, h)

    def finish_keys(h):
        total = xk[h, 0].astype(jnp.float32)
        for j in range(1, nx):
            landed(rx.at[h, j - 1], oxr.at[h, j - 1], xpeer[j])
            total = total + rx[h, j - 1].astype(jnp.float32)
        fin[h, 2] = total[0].astype(jnp.bfloat16)
        fin[h, 3] = total[1].astype(jnp.bfloat16)
        hand_back(1, h)

    def tables_in():
        for load in tables:
            load.wait()
        mask_parts()

    steps = {
        "U": functools.partial(scatter, 0), "V": functools.partial(scatter, 1),
        "q": spread_queries, "p": spread_keys, "F": forward, "a": own_scores, "A": first_pass,
        "B": second_pass, "K": core_sum, "X": finish_queries, "Y": finish_keys,
    }
    for step in ORDER:
        if step == "M":
            tables_in()
        else:
            steps[step[0]](int(step[1]))
    for copy in sum(leaving, sent):
        copy.wait_send()
    for h in range(NH):
        for part in range(2):
            for j in range(1, nz):
                landed(
                    out.at[pl.ds(2 * part, 2), :, columns((z + j) % nz, h)],
                    zr.at[part, h, j - 1], zpeer[j],
                )


def deliver(done, att_out, dq_out, dk_out, dv_out, sem):
    stores = [
        pltpu.make_async_copy(done.at[i], dst, sem.at[i])
        for i, dst in enumerate((att_out, dq_out, dk_out, dv_out))
    ]
    for store in stores:
        store.start()
    for store in stores:
        store.wait()


def on_device(nz, nx, ny, queries, keys, values, out_grad, tile_mask, span_order):
    width = queries.shape[1]
    blk = nz * TOK
    qt, kt = ny * blk, 2 * nx * blk
    bf, f32 = jnp.bfloat16, jnp.float32
    dma = pltpu.SemaphoreType.DMA
    vmem = pl.BlockSpec(memory_space=pltpu.VMEM)
    hbm = pl.BlockSpec(memory_space=pltpu.HBM)
    done = pl.pallas_call(
        functools.partial(kernel, nz, nx, ny),
        out_shape=pltpu.VMEM((4, TOK, width), bf),
        in_specs=[hbm] * 6,
        out_specs=vmem,
        scratch_shapes=[
            pltpu.VMEM(tile_mask.shape, jnp.int32),
            pltpu.VMEM((1, tile_mask.shape[0]), jnp.int32),
            pltpu.VMEM((4, TOK, width), bf),
            pltpu.VMEM((NH, 4, kt, HD), bf),
            pltpu.VMEM((kt, HD), bf),
            pltpu.VMEM((qt, HD), bf),
            pltpu.VMEM((NH, kt, qt), f32),
            pltpu.VMEM((NH, kt, qt), f32),
            pltpu.VMEM((kt, qt), bf),
            pltpu.VMEM((kt, qt), bf),
            pltpu.VMEM((NH, ny, -(-3 * ny // 8) * 8, blk), f32),
            pltpu.VMEM((NH, ny, 2, HD, blk), bf),
            pltpu.VMEM((NH, ny - 1, 2, HD, blk), bf),
            pltpu.VMEM((NH, 2, nx, 2, blk, HD), bf),
            pltpu.VMEM((NH, nx, 2, blk, HD), bf),
            pltpu.VMEM((NH, nx, 2, blk, HD), bf),
            pltpu.VMEM((NH, nx - 1, 2, blk, HD), bf),
            pltpu.VMEM((NH, 4, blk, HD), bf),
            dma((6,)), dma((2, NH)),
            dma((2, NH, nz - 1)), dma((2, NH, nz - 1)),
            dma((NH, ny - 1)), dma((NH, ny - 1)),
            dma((NH, nx - 1)), dma((NH, nx - 1)),
            dma((NH, nx)), dma((NH, nx)),
            dma((NH, ny - 1)), dma((NH, ny - 1)),
            dma((NH, ny - 1)), dma((NH, ny - 1)),
            dma((NH,)), dma((NH,)),
            dma((NH, nx - 1)), dma((NH, nx - 1)),
            dma((2, NH, nz - 1)), dma((2, NH, nz - 1)),
        ],
        compiler_params=pltpu.CompilerParams(
            collective_id=0, has_side_effects=True, vmem_limit_bytes=48 * 1024 * 1024
        ),
    )(
        *[
            pltpu.with_memory_space_constraint(a, pltpu.HBM)
            for a in (queries, keys, values, out_grad, tile_mask, span_order.reshape(1, -1))
        ]
    )
    outs = pl.pallas_call(
        deliver,
        out_shape=[pltpu.HBM(queries.shape, bf)] * 4,
        in_specs=[pl.BlockSpec(memory_space=pl.ANY)],
        out_specs=[hbm] * 4,
        scratch_shapes=[dma((4,))],
        compiler_params=pltpu.CompilerParams(vmem_limit_bytes=1024 * 1024),
    )(pltpu.with_memory_space_constraint(done, pltpu.VMEM))
    return tuple(outs)


def solution(mesh, nx=X_CHIPS):
    nz, ny = mesh.shape["ctx"] // nx, mesh.shape["head"] // 2
    rows = P(("ctx", "head"), None)
    return jax.shard_map(
        functools.partial(on_device, nz, nx, ny),
        mesh=mesh,
        in_specs=(rows, rows, rows, rows, P(), P()),
        out_specs=(rows, rows, rows, rows),
        check_vma=False,
    )
```

```python
import functools
import math

import jax
import jax.numpy as jnp
from jax import lax
from jax.experimental import pallas as pl
from jax.experimental.pallas import tpu as pltpu
from jax.sharding import PartitionSpec as P

HD = 128
SPAN = 64
TOK = 16
NH = 3
X_CHIPS = 4
BIG = 2.0**100
FLOOR = -(2.0**80)
MESH = pl.DeviceIdType.MESH
CHUNK = 256
UNROLL = 2
ORDER = (
    "V0", "U0", "M", "V1", "p0", "V2", "q0", "U1", "p1", "U2", "F0", "p2",
    "q1", "q2", "a0", "A0", "F1", "a1", "A1", "F2", "B0", "a2", "K0", "A2",
    "B1", "X0", "K1", "B2", "K2", "Y0", "X1", "Y1", "X2", "Y2",
)


def dot_last(a, b):
    return lax.dot_general(a, b, (((1,), (1,)), ((), ())), preferred_element_type=jnp.float32)


def dot_first(a, b):
    return lax.dot_general(a, b, (((0,), (0,)), ((), ())), preferred_element_type=jnp.float32)


def dot(a, b):
    return lax.dot_general(a, b, (((1,), (0,)), ((), ())), preferred_element_type=jnp.float32)


def rows8(a):
    return a.reshape(a.shape[0] // 8, 8, a.shape[1])


def kernel(
    nz, nx, ny,
    q_in, k_in, v_in, g_in, mask_in, span_in,
    out,
    mask_ref, span_ref, inb, buf, key_hot, bias, probs, dprob, pb, ds, stat, oq, rq, ok, rs, xk, rx, fin,
    io_sem, own_sem,
    s1s, s1r, ys, yr, xs, xr, cs, cr, ts, tr, oys, oyr, ocs, ocr, oxs, oxr, zs, zr,
):
    blk = nz * TOK
    qt, kt = ny * blk, 2 * nx * blk
    chunk = min(CHUNK, nx * blk)
    hw = NH * HD
    spans = mask_ref.shape[0]
    scale = HD**-0.5
    log2e = scale * math.log2(math.e)
    ctx, head = lax.axis_index("ctx"), lax.axis_index("head")
    z, x = ctx // nx, ctx % nx
    y, c = head // 2, head % 2
    zpeer = [(((z + j) % nz) * nx + x, head) for j in range(nz)]
    xpeer = [(z * nx + (x + j) % nx, head) for j in range(nx)]
    ypeer = [(ctx, ((y + j) % ny) * 2 + c) for j in range(ny)]
    sibling = (ctx, y * 2 + (1 - c))

    def remote(src, dst, send, recv, device):
        return pltpu.make_async_remote_copy(
            src_ref=src, dst_ref=dst, send_sem=send, recv_sem=recv,
            device_id=device, device_id_type=MESH,
        )

    def landed(dst, recv, device):
        remote(dst, dst, recv, recv, device).wait_recv()

    def columns(pos, h):
        return pl.ds(pl.multiple_of(pos * hw + h * HD, HD), HD)

    loads = [
        pltpu.make_async_copy(src, inb.at[i], io_sem.at[i])
        for i, src in enumerate((q_in, g_in, k_in, v_in))
    ]
    tables = [
        pltpu.make_async_copy(mask_in, mask_ref, io_sem.at[4]),
        pltpu.make_async_copy(span_in, span_ref, io_sem.at[5]),
    ]
    barrier = pltpu.get_barrier_semaphore()
    peers = zpeer[1:] + xpeer[1:] + ypeer[1:] + [sibling]
    for peer in peers:
        pl.semaphore_signal(barrier, inc=1, device_id=peer, device_id_type=MESH)
    for load in loads + tables:
        load.start()
    pl.semaphore_wait(barrier, len(peers))
    for load in loads:
        load.wait()

    sent, leaving = [], []

    def go(*args):
        copy = remote(*args)
        copy.start()
        sent.append(copy)

    def own_tokens(part, h):
        return pltpu.make_async_copy(
            inb.at[pl.ds(2 * part, 2), :, columns(z, h)],
            buf.at[h, pl.ds(2 * part, 2), pl.ds(0, TOK), :],
            own_sem.at[part, h],
        )

    def scatter(part, h):
        if len(leaving) == 2:
            for copy in leaving.pop(0):
                copy.wait_send()
        piece = []
        for j in range(1, nz):
            copy = remote(
                inb.at[pl.ds(2 * part, 2), :, columns((z + j) % nz, h)],
                buf.at[h, pl.ds(2 * part, 2), pl.ds((nz - j) * TOK, TOK), :],
                s1s.at[part, h, j - 1], s1r.at[part, h, nz - j - 1], zpeer[j],
            )
            copy.start()
            piece.append(copy)
        leaving.append(piece)
        own_tokens(part, h).start()

    def gathered(part, h):
        own_tokens(part, h).wait()
        for j in range(1, nz):
            landed(
                buf.at[h, pl.ds(2 * part, 2), pl.ds(j * TOK, TOK), :],
                s1r.at[part, h, j - 1], zpeer[j],
            )
        return buf.at[h, pl.ds(2 * part, 2), pl.ds(0, blk), :]

    def spread_queries(h):
        qg = gathered(0, h)
        for j in range(1, ny):
            go(
                qg, buf.at[h, pl.ds(0, 2), pl.ds((ny - j) * blk, blk), :],
                ys.at[h, j - 1], yr.at[h, ny - j - 1], ypeer[j],
            )

    def spread_keys(h):
        kv = gathered(1, h)
        for j in range(1, nx):
            go(
                kv, buf.at[h, pl.ds(2, 2), pl.ds((nx - j) * blk, blk), :],
                xs.at[h, j - 1], xr.at[h, nx - j - 1], xpeer[j],
            )
        go(
            kv, buf.at[h, pl.ds(2, 2), pl.ds(nx * blk, blk), :],
            cs.at[h, 0], cr.at[h, 0], sibling,
        )

    def forward(h):
        for j in range(1, nx):
            here = buf.at[h, pl.ds(2, 2), pl.ds(j * blk, blk), :]
            landed(here, xr.at[h, j - 1], xpeer[j])
            go(
                here, buf.at[h, pl.ds(2, 2), pl.ds((nx + j) * blk, blk), :],
                cs.at[h, j], cr.at[h, j], sibling,
            )

    def span_of(zz, xx, yy):
        return lax.div(((zz * nx + xx) * ny + yy) * 2 * TOK, SPAN)

    def mask_parts():
        tile = span_ref[...]
        picks = (lax.broadcasted_iota(jnp.int32, (spans, spans), 0) == tile).astype(jnp.bfloat16)
        table = mask_ref[...].astype(jnp.float32).astype(jnp.bfloat16)
        table = dot(table, picks).astype(jnp.bfloat16)
        table = dot_first(picks, table).astype(jnp.bfloat16)
        row = lax.broadcasted_iota(jnp.int32, (qt, spans), 0)
        slot, zz = lax.div(row, blk), lax.rem(lax.div(row, TOK), nz)
        span = span_of(lax.rem(zz + z, nz), x, lax.rem(slot + y, ny))
        hot = (lax.broadcasted_iota(jnp.int32, (qt, spans), 1) == span).astype(jnp.bfloat16)
        reach = dot(hot, table)
        bias[...] = jnp.zeros_like(bias)
        bias[:, pl.ds(0, spans)] = jnp.where(reach > 0.5, 0.0, -BIG).astype(jnp.bfloat16)
        row = lax.broadcasted_iota(jnp.int32, (kt, HD), 0)
        slot, zz = lax.rem(lax.div(row, blk), nx), lax.rem(lax.div(row, TOK), nz)
        span = span_of(lax.rem(zz + z, nz), lax.rem(slot + x, nx), y)
        key_hot[...] = (lax.broadcasted_iota(jnp.int32, (kt, HD), 1) == span).astype(
            jnp.float32
        ).astype(jnp.bfloat16)

    half = kt // 2
    tops = {}

    def chunks(first, body, carry):
        def step(i, carry):
            return body(pl.ds(pl.multiple_of(first + i * chunk, chunk), chunk), carry)

        return lax.fori_loop(0, half // chunk, step, carry, unroll=UNROLL)

    def scores(h, first, top):
        query = jnp.concatenate([buf[h, 0, pl.ds(0, qt), :], bias[...]], axis=1)
        cotangent = buf[h, 1, pl.ds(0, qt), :]

        def body(at, top):
            key = jnp.concatenate([buf[h, 2, at, :], key_hot[at, :]], axis=1)
            s = dot_last(key, query)
            probs[h, at, :] = s
            dprob[h, at, :] = dot_last(buf[h, 3, at, :], cotangent)
            return jnp.maximum(top, jnp.max(rows8(s), axis=0))

        return chunks(first, body, top)

    def own_scores(h):
        for j in range(1, ny):
            landed(buf.at[h, pl.ds(0, 2), pl.ds(j * blk, blk), :], yr.at[h, j - 1], ypeer[j])
        tops[h] = scores(h, 0, jnp.full((8, qt), FLOOR, jnp.float32))

    def first_pass(h):
        for j in range(nx):
            landed(buf.at[h, pl.ds(2, 2), pl.ds((nx + j) * blk, blk), :], cr.at[h, j], sibling)
        top = jnp.max(scores(h, half, tops.pop(h)), axis=0, keepdims=True)

        def body(at, carry):
            total, inner = carry
            p = jnp.exp2((probs[h, at, :] - top) * log2e)
            probs[h, at, :] = p
            return (
                total + jnp.sum(rows8(p), axis=0),
                inner + jnp.sum(rows8(p * dprob[h, at, :]), axis=0),
            )

        zero = jnp.zeros((8, qt), jnp.float32)
        total, inner = chunks(half, body, chunks(0, body, (zero, zero)))
        total, inner = [jnp.sum(a, axis=0, keepdims=True) for a in (total, inner)]
        rows = [a[:, k * blk : (k + 1) * blk] for a in (top, total, inner) for k in range(ny)]
        rows += [jnp.zeros((stat.shape[2] - 3 * ny, blk), jnp.float32)]
        stat[h, 0] = jnp.concatenate(rows, axis=0)
        for j in range(1, ny):
            go(
                stat.at[h, 0], stat.at[h, ny - j],
                ts.at[h, j - 1], tr.at[h, ny - j - 1], ypeer[j],
            )

    def second_pass(h):
        for j in range(1, ny):
            landed(stat.at[h, j], tr.at[h, j - 1], ypeer[j])
        def rows(j, kind):
            return jnp.concatenate(
                [stat[h, j, pl.ds(kind * ny + (k - j) % ny, 1), :] for k in range(ny)], axis=1
            )

        peaks = [rows(j, 0) for j in range(ny)]
        top = functools.reduce(jnp.maximum, peaks)
        shares = [jnp.exp2((peak - top) * log2e) for peak in peaks]
        total = sum(w * rows(j, 1) for j, w in enumerate(shares))
        delta = sum(w * rows(j, 2) for j, w in enumerate(shares)) / total
        norm = shares[0] / total

        query, cotangent = buf[h, 0, pl.ds(0, qt), :], buf[h, 1, pl.ds(0, qt), :]

        def key_side(core):
            for i in range(half // chunk):
                at = pl.ds(core * half + i * chunk, chunk)
                p = probs[h, at, :] * norm
                p_low = p.astype(jnp.bfloat16)
                dscore = (p * (dprob[h, at, :] - delta)).astype(jnp.bfloat16)
                pb[at, :] = p_low
                ds[at, :] = dscore
                dk = (dot(dscore, query) * scale).astype(jnp.bfloat16)
                dv = dot(p_low, cotangent).astype(jnp.bfloat16)
                for j in range(chunk // blk):
                    ok[h, core, i * (chunk // blk) + j, 0] = dk[j * blk : (j + 1) * blk]
                    ok[h, core, i * (chunk // blk) + j, 1] = dv[j * blk : (j + 1) * blk]

        key_side(1)
        go(ok.at[h, 1], rs.at[h], ocs.at[h], ocr.at[h], sibling)
        key_side(0)
        att = dot_first(buf[h, 3], pb[...]).astype(jnp.bfloat16)
        dq = (dot_first(buf[h, 2], ds[...]) * scale).astype(jnp.bfloat16)
        for j in range(ny):
            oq[h, j, 0] = att[:, j * blk : (j + 1) * blk]
            oq[h, j, 1] = dq[:, j * blk : (j + 1) * blk]
        for j in range(1, ny):
            go(
                oq.at[h, j], rq.at[h, ny - j - 1],
                oys.at[h, j - 1], oyr.at[h, ny - j - 1], ypeer[j],
            )

    def core_sum(h):
        landed(rs.at[h], ocr.at[h], sibling)
        for j in range(nx):
            both = ok[h, 0, j].astype(jnp.float32) + rs[h, j].astype(jnp.float32)
            xk[h, j] = both.astype(jnp.bfloat16)
        for j in range(1, nx):
            go(
                xk.at[h, j], rx.at[h, nx - j - 1],
                oxs.at[h, j - 1], oxr.at[h, nx - j - 1], xpeer[j],
            )

    def hand_back(part, h):
        for j in range(1, nz):
            go(
                fin.at[h, pl.ds(2 * part, 2), pl.ds(j * TOK, TOK), :],
                out.at[pl.ds(2 * part, 2), :, columns(z, h)],
                zs.at[part, h, j - 1], zr.at[part, h, nz - j - 1], zpeer[j],
            )
        out[pl.ds(2 * part, 2), :, columns(z, h)] = fin[h, pl.ds(2 * part, 2), pl.ds(0, TOK), :]

    def finish_queries(h):
        total = oq[h, 0].astype(jnp.float32)
        for j in range(1, ny):
            landed(rq.at[h, j - 1], oyr.at[h, j - 1], ypeer[j])
            total = total + rq[h, j - 1].astype(jnp.float32)
        fin[h, 0] = total[0].T.astype(jnp.bfloat16)
        fin[h, 1] = total[1].T.astype(jnp.bfloat16)
        hand_back(0, h)

    def finish_keys(h):
        total = xk[h, 0].astype(jnp.float32)
        for j in range(1, nx):
            landed(rx.at[h, j - 1], oxr.at[h, j - 1], xpeer[j])
            total = total + rx[h, j - 1].astype(jnp.float32)
        fin[h, 2] = total[0].astype(jnp.bfloat16)
        fin[h, 3] = total[1].astype(jnp.bfloat16)
        hand_back(1, h)

    def tables_in():
        for load in tables:
            load.wait()
        mask_parts()

    steps = {
        "U": functools.partial(scatter, 0), "V": functools.partial(scatter, 1),
        "q": spread_queries, "p": spread_keys, "F": forward, "a": own_scores, "A": first_pass,
        "B": second_pass, "K": core_sum, "X": finish_queries, "Y": finish_keys,
    }
    for step in ORDER:
        if step == "M":
            tables_in()
        else:
            steps[step[0]](int(step[1]))
    for copy in sum(leaving, sent):
        copy.wait_send()
    for h in range(NH):
        for part in range(2):
            for j in range(1, nz):
                landed(
                    out.at[pl.ds(2 * part, 2), :, columns((z + j) % nz, h)],
                    zr.at[part, h, j - 1], zpeer[j],
                )


def deliver(done, att_out, dq_out, dk_out, dv_out, sem):
    stores = [
        pltpu.make_async_copy(done.at[i], dst, sem.at[i])
        for i, dst in enumerate((att_out, dq_out, dk_out, dv_out))
    ]
    for store in stores:
        store.start()
    for store in stores:
        store.wait()


def on_device(nz, nx, ny, queries, keys, values, out_grad, tile_mask, span_order):
    width = queries.shape[1]
    blk = nz * TOK
    qt, kt = ny * blk, 2 * nx * blk
    bf, f32 = jnp.bfloat16, jnp.float32
    dma = pltpu.SemaphoreType.DMA
    vmem = pl.BlockSpec(memory_space=pltpu.VMEM)
    hbm = pl.BlockSpec(memory_space=pltpu.HBM)
    done = pl.pallas_call(
        functools.partial(kernel, nz, nx, ny),
        out_shape=pltpu.VMEM((4, TOK, width), bf),
        in_specs=[hbm] * 6,
        out_specs=vmem,
        scratch_shapes=[
            pltpu.VMEM(tile_mask.shape, jnp.int32),
            pltpu.VMEM((1, tile_mask.shape[0]), jnp.int32),
            pltpu.VMEM((4, TOK, width), bf),
            pltpu.VMEM((NH, 4, kt, HD), bf),
            pltpu.VMEM((kt, HD), bf),
            pltpu.VMEM((qt, HD), bf),
            pltpu.VMEM((NH, kt, qt), f32),
            pltpu.VMEM((NH, kt, qt), f32),
            pltpu.VMEM((kt, qt), bf),
            pltpu.VMEM((kt, qt), bf),
            pltpu.VMEM((NH, ny, -(-3 * ny // 8) * 8, blk), f32),
            pltpu.VMEM((NH, ny, 2, HD, blk), bf),
            pltpu.VMEM((NH, ny - 1, 2, HD, blk), bf),
            pltpu.VMEM((NH, 2, nx, 2, blk, HD), bf),
            pltpu.VMEM((NH, nx, 2, blk, HD), bf),
            pltpu.VMEM((NH, nx, 2, blk, HD), bf),
            pltpu.VMEM((NH, nx - 1, 2, blk, HD), bf),
            pltpu.VMEM((NH, 4, blk, HD), bf),
            dma((6,)), dma((2, NH)),
            dma((2, NH, nz - 1)), dma((2, NH, nz - 1)),
            dma((NH, ny - 1)), dma((NH, ny - 1)),
            dma((NH, nx - 1)), dma((NH, nx - 1)),
            dma((NH, nx)), dma((NH, nx)),
            dma((NH, ny - 1)), dma((NH, ny - 1)),
            dma((NH, ny - 1)), dma((NH, ny - 1)),
            dma((NH,)), dma((NH,)),
            dma((NH, nx - 1)), dma((NH, nx - 1)),
            dma((2, NH, nz - 1)), dma((2, NH, nz - 1)),
        ],
        compiler_params=pltpu.CompilerParams(
            collective_id=0, has_side_effects=True, vmem_limit_bytes=48 * 1024 * 1024
        ),
    )(
        *[
            pltpu.with_memory_space_constraint(a, pltpu.HBM)
            for a in (queries, keys, values, out_grad, tile_mask, span_order.reshape(1, -1))
        ]
    )
    outs = pl.pallas_call(
        deliver,
        out_shape=[pltpu.HBM(queries.shape, bf)] * 4,
        in_specs=[pl.BlockSpec(memory_space=pl.ANY)],
        out_specs=[hbm] * 4,
        scratch_shapes=[dma((4,))],
        compiler_params=pltpu.CompilerParams(vmem_limit_bytes=1024 * 1024),
    )(pltpu.with_memory_space_constraint(done, pltpu.VMEM))
    return tuple(outs)


def solution(mesh, nx=X_CHIPS):
    nz, ny = mesh.shape["ctx"] // nx, mesh.shape["head"] // 2
    rows = P(("ctx", "head"), None)
    return jax.shard_map(
        functools.partial(on_device, nz, nx, ny),
        mesh=mesh,
        in_specs=(rows, rows, rows, rows, P(), P()),
        out_specs=(rows, rows, rows, rows),
        check_vma=False,
    )
```
